512 devices in a mesh: ctx: 32 (over z_hi, x, core), dp: 16 (over z_lo, y).
Axes of the slice: x: 4, y: 4, z: 16 (z_hi: 4, z_lo: 4; z = z_hi * 4 + z_lo), core: 2. Of those that a mesh axis runs over, the one named last changes fastest.
Arguments:
- queries: bfloat16 [16, 4096, 4096], P('dp', 'ctx'), may hold values from -4.5 to 4.5
- key_heads: bfloat16 [16, 4096, 512], P('dp', 'ctx'), may hold values from -4.5 to 4.5
- value_heads: bfloat16 [16, 4096, 512], P('dp', 'ctx'), may hold values from -6 to 6
- out_grad: bfloat16 [16, 4096, 4096], P('dp', 'ctx'), may hold values from -6 to 6
- block_order: int32 [64], replicated, may hold values from 0 to 63, each once
Outputs:
- attn_out: bfloat16 [16, 4096, 4096], P('dp', 'ctx')
- dqueries: bfloat16 [16, 4096, 4096], P('dp', 'ctx')
- dkey_heads: bfloat16 [16, 4096, 512], P('dp', 'ctx')
- dvalue_heads: bfloat16 [16, 4096, 512], P('dp', 'ctx')
- out_factor: float32 [4096, 128], P(('ctx', 'dp'))
- grad_factor: float32 [1024, 256], P(('ctx', 'dp'))
The draws below stay inside these ranges and needn't reach their ends.
Inputs may be any that keep to these rules, and one draw needn't show every extreme that they name: Slot b lies on ctx index b // 2 (the first 64 tokens for even b, the last 64 for odd b) and holds positions block_order[b] * 64 to block_order[b] * 64 + 63 of every sequence; each value appears once.
All inputs are finite; a program needn't handle non-finite values.
Results may differ from the reference program's by a relative error of at most 0.025.
Values may be sent and summed in bfloat16 or wider, within the bound.
A program may use at most 128 MiB of HBM per device.

```python
import math
import jax
import jax.numpy as jnp
from jax import lax

H = 32
KVH = 4
HD = 128
STEPS = 4
TOK_DEV = 128
HALF = 64
CTX_DEVS = 32
BLOCKS = 64
SEQS = 16
LENGTH = 4096


def draw_queries(key, part):
    key = jax.random.fold_in(key, 1)
    return jax.random.truncated_normal(key, -4.5, 4.5, (SEQS, LENGTH, H * HD), jnp.float32).astype(jnp.bfloat16)


def draw_key_heads(key, part):
    key = jax.random.fold_in(key, 5)
    return jax.random.truncated_normal(key, -4.5, 4.5, (SEQS, LENGTH, KVH * HD), jnp.float32).astype(jnp.bfloat16)


def raised(result, stream_key, source, target, parts, factor):
    def block_of(dim):
        return (jnp.arange(result.shape[dim]) // (result.shape[dim] // parts)).reshape((-1,) + (1,) * (result.ndim - 1 - dim))

    one_side = jax.random.permutation(stream_key, parts)[block_of(target)]
    second = (block_of(target) + parts // 2) % parts
    return jnp.where((block_of(source) == one_side) | (block_of(source) == second), factor * result, result)


def levels(stream_key, dims, cuts, smallest, top_value):
    factor_of = 1.0
    for position, blocks in cuts:
        draws = jax.random.uniform(jax.random.fold_in(jax.random.fold_in(stream_key, 6), position), (blocks,), jnp.float32, smallest / len(cuts), top_value / len(cuts))
        factor_of = factor_of * jnp.repeat(jnp.exp(draws), dims[position] // blocks).reshape((-1,) + (1,) * (len(dims) - 1 - position))
    return factor_of


def bell_draw(key, dims, scale, most, split=(), kind=jnp.bfloat16):
    entries = scale * jax.random.normal(key, dims, jnp.float32)
    if split:
        entries = entries * levels(key, dims, split, -0.22, 0.18)
    return jnp.clip(entries, -most, most).astype(kind)


def noise_with(stream_key, dims, spread, most, split, heavy, kind=jnp.bfloat16):
    array = spread * jax.random.normal(stream_key, dims, jnp.float32)
    if split:
        array = array * levels(stream_key, dims, split, -0.22, 0.18)
    return jnp.clip(raised(array, jax.random.fold_in(stream_key, 3), *heavy), -most, most).astype(kind)


def setup_inputs(seed: int = 0) -> dict:
    key_of = jax.random.split(jax.random.key(seed), 6)
    return {
        "queries": draw_queries(jax.random.fold_in(key_of[5], 71), 0),
        "key_heads": draw_key_heads(jax.random.fold_in(key_of[5], 71), 0),
        "value_heads": bell_draw(key_of[2], (SEQS, LENGTH, KVH * HD), 1.0, 6.0, ((0, 16), (1, 32))),
        "out_grad": noise_with(key_of[3], (SEQS, LENGTH, H * HD), 1.0, 6.0, ((0, 16), (1, 32)), (1, 2, 32, 2.75)),
        "block_order": jax.random.permutation(key_of[4], BLOCKS).astype(jnp.int32),
    }


def hold_round(tensor):
    return lax.optimization_barrier(tensor.astype(jnp.bfloat16)).astype(jnp.float32)

def places(block_order):
    halves = block_order.reshape(CTX_DEVS, 2)
    offsets = jnp.arange(HALF, dtype=jnp.int32)
    return (halves[:, :, None] * HALF + offsets[None, None, :]).reshape(CTX_DEVS, TOK_DEV).astype(jnp.int32)

def block_scores(query_all, key_blocks, key_places, query_places, scaling):
    visible = key_places[:, None, :] <= query_places[:, :, None]
    scores = jnp.einsum('ctgjd,cugd->cgjtu', query_all, key_blocks, precision=lax.Precision.HIGHEST) * scaling
    return (visible[:, None, None, :, :], scores)

def one_sequence(query_seq, key_seq, value_seq, grad_seq, query_places):
    group_size = H // KVH
    scaling = jnp.float32(1.0 / math.sqrt(HD))
    query_all = query_seq.astype(jnp.float32).reshape(CTX_DEVS, TOK_DEV, KVH, group_size, HD)
    grad_all = grad_seq.astype(jnp.float32).reshape(CTX_DEVS, TOK_DEV, KVH, group_size, HD)
    key_all = key_seq.astype(jnp.float32).reshape(CTX_DEVS, TOK_DEV, KVH, HD)
    value_all = value_seq.astype(jnp.float32).reshape(CTX_DEVS, TOK_DEV, KVH, HD)
    maxima, totals, weighted = ([], [], [])
    for visit_index in range(STEPS):
        key_blocks = jnp.roll(key_all, visit_index, axis=0)
        value_blocks = jnp.roll(value_all, visit_index, axis=0)
        key_places = jnp.roll(query_places, visit_index, axis=0)
        visible, scores = block_scores(query_all, key_blocks, key_places, query_places, scaling)
        block_max = lax.optimization_barrier(jnp.max(jnp.where(visible, scores, -jnp.inf), axis=-1))
        has_key = jnp.any(visible, axis=-1)
        safe_max = jnp.where(has_key, block_max, 0.0)
        block_weights = hold_round(jnp.where(visible, jnp.exp(scores - safe_max[..., None]), 0.0))
        totals.append(lax.optimization_barrier(jnp.sum(block_weights, axis=-1)))
        weighted.append(jnp.einsum('cgjtu,cugd->cgjtd', block_weights, value_blocks, precision=lax.Precision.HIGHEST))
        maxima.append(jnp.where(has_key, block_max, -jnp.inf))
    upper_max = maxima[0]
    for block_entry in maxima[1:]:
        upper_max = jnp.maximum(upper_max, block_entry)
    norm_total = jnp.zeros_like(upper_max)
    mixed_sum = jnp.zeros_like(weighted[0])
    for visit_index in range(STEPS):
        factor = jnp.exp(maxima[visit_index] - upper_max)
        norm_total = norm_total + factor * totals[visit_index]
        mixed_sum = mixed_sum + factor[..., None] * weighted[visit_index]
    attn_rows = hold_round(jnp.transpose(mixed_sum / norm_total[..., None], (0, 3, 1, 2, 4)))
    log_total = upper_max + jnp.log(norm_total)
    delta_rows = jnp.transpose(lax.optimization_barrier(jnp.sum(grad_all * attn_rows, axis=-1)), (0, 2, 3, 1))
    dquery_sum = jnp.zeros_like(query_all)
    dkey_sum = jnp.zeros_like(key_all)
    dvalue_sum = jnp.zeros_like(value_all)
    for visit_index in range(STEPS):
        key_blocks = jnp.roll(key_all, visit_index, axis=0)
        value_blocks = jnp.roll(value_all, visit_index, axis=0)
        key_places = jnp.roll(query_places, visit_index, axis=0)
        visible, scores = block_scores(query_all, key_blocks, key_places, query_places, scaling)
        prob_full = jnp.where(visible, jnp.exp(scores - log_total[..., None]), 0.0)
        prob_round = hold_round(prob_full)
        dvalue_part = jnp.einsum('cgjtu,ctgjd->cugd', prob_round, grad_all, precision=lax.Precision.HIGHEST)
        dprob_full = jnp.einsum('ctgjd,cugd->cgjtu', grad_all, value_blocks, precision=lax.Precision.HIGHEST)
        dscore = hold_round(prob_full * (dprob_full - delta_rows[..., None]))
        dquery_sum = dquery_sum + jnp.einsum('cgjtu,cugd->ctgjd', dscore, key_blocks, precision=lax.Precision.HIGHEST)
        dkey_part = jnp.einsum('cgjtu,ctgjd->cugd', dscore, query_all, precision=lax.Precision.HIGHEST)
        dkey_sum = dkey_sum + jnp.roll(dkey_part, -visit_index, axis=0)
        dvalue_sum = dvalue_sum + jnp.roll(dvalue_part, -visit_index, axis=0)
    dquery_round = (dquery_sum * scaling).astype(jnp.bfloat16)
    dkey_round = (dkey_sum * scaling).astype(jnp.bfloat16)
    dvalue_round = dvalue_sum.astype(jnp.bfloat16)
    out_rows = attn_rows.reshape(LENGTH, H, HD)
    out_gram = jnp.einsum('thd,the->hde', out_rows, out_rows, precision=lax.Precision.HIGHEST)
    joined = jnp.concatenate([lax.optimization_barrier(dkey_round).astype(jnp.float32).reshape(LENGTH, KVH, HD), lax.optimization_barrier(dvalue_round).astype(jnp.float32).reshape(LENGTH, KVH, HD)], axis=2)
    grad_gram = jnp.einsum('tgd,tge->gde', joined, joined, precision=lax.Precision.HIGHEST)
    return (attn_rows.astype(jnp.bfloat16).reshape(LENGTH, H * HD), dquery_round.reshape(LENGTH, H * HD), dkey_round.reshape(LENGTH, KVH * HD), dvalue_round.reshape(LENGTH, KVH * HD), out_gram, grad_gram)

def reference(queries, key_heads, value_heads, out_grad, block_order):
    query_places = places(block_order)

    def per_sequence(sequence):
        return one_sequence(sequence[0], sequence[1], sequence[2], sequence[3], query_places)
    outputs = lax.map(per_sequence, (queries, key_heads, value_heads, out_grad))
    attn_out, dqueries, dkey_heads, dvalue_heads, out_grams, grad_grams = outputs
    token_total = SEQS * LENGTH
    out_factor = (lax.optimization_barrier(jnp.sum(out_grams, axis=0)) / token_total).reshape(H * HD, HD)
    grad_factor = (lax.optimization_barrier(jnp.sum(grad_grams, axis=0)) / token_total).reshape(KVH * 2 * HD, 2 * HD)
    return (attn_out, dqueries, dkey_heads, dvalue_heads, out_factor, grad_factor)
```

```python
import math

import jax
import jax.numpy as jnp
from jax import lax
from jax.experimental import pallas as pl
from jax.experimental.pallas import tpu as pltpu
from jax.sharding import PartitionSpec as P

HD = 128
STEPS = 4
TOK = 128
KVH = 4
NEG = -1e30
LOG2E = 1.0 / math.log(2.0)
SCALE = 1.0 / math.sqrt(HD)
MESH = pl.DeviceIdType.MESH
BF = jnp.bfloat16
F32 = jnp.float32


def dot(a, b, ca, cb):
    return lax.dot_general(a, b, (((ca,), (cb,)), ((), ())), preferred_element_type=F32)


class Place:
    def __init__(self):
        c, d = lax.axis_index("ctx"), lax.axis_index("dp")
        self.zh, self.x, self.core = c // 8, (c % 8) // 2, c % 2
        self.zl, self.y = d // 4, d % 4

    def at(self, x=None, core=None, y=None, zl=None, zh=None):
        x = self.x if x is None else x
        core = self.core if core is None else core
        y = self.y if y is None else y
        zl = self.zl if zl is None else zl
        zh = self.zh if zh is None else zh
        return (zh * 8 + x * 2 + core, zl * 4 + y)


def both(*conds):
    total = conds[0]
    for cond in conds[1:]:
        total = jnp.logical_and(total, cond)
    return total


class Sends:
    def __init__(self, sems):
        self.sems, self.count, self.open = sems, 0, []

    def start(self, cond, src, dst, recv_sem, device):
        copy = pltpu.make_async_remote_copy(
            src_ref=src, dst_ref=dst, send_sem=self.sems.at[self.count], recv_sem=recv_sem,
            device_id=device, device_id_type=MESH,
        )
        self.count += 1
        self.open.append((cond, copy))
        if cond is None:
            copy.start()
        else:
            pl.when(cond)(copy.start)

    def finish(self):
        for cond, copy in self.open:
            if cond is None:
                copy.wait_send()
            else:
                pl.when(cond)(copy.wait_send)
        self.open = []


def arrived(dst, sem):
    pltpu.make_async_copy(dst, dst, sem).wait()


def signal(cond, sem, device):
    def act():
        pl.semaphore_signal(sem, inc=1, device_id=device, device_id_type=MESH)
    if cond is None:
        act()
    else:
        pl.when(cond)(act)


def number(cond):
    return jnp.where(cond, 1, 0).astype(jnp.int32)


def gather_kernel(k_ref, v_ref, kv_ref, rel, ssem, rsem, relsem, lsem):
    p = Place()
    x, core = p.x, p.core
    own = (k_ref, v_ref)
    up, down = (p.zh + 1) % 4, (p.zh + 3) % 4
    owner = jnp.logical_or(x == 3, both(x == 2, core == 1))
    blk = 2 * (x - 2) + core - 1
    owners = ((2, 1, 0), (3, 0, 1), (3, 1, 2))

    bar = pltpu.get_barrier_semaphore()
    signal(None, bar, p.at(core=1 - core))
    for c2 in range(2):
        signal(x >= 1, bar, p.at(x=x - 1, core=c2))
    signal(both(x >= 2, core == 0), bar, p.at(x=x - 2, core=1))
    for ox, oc, b in owners:
        signal(jnp.logical_not(both(x == ox, core == oc)), bar, p.at(x=ox, core=oc))
    for j in range(4):
        signal(x == 0, bar, p.at(x=j, zh=down))
        signal(both(x == 0, core == 0), bar, p.at(x=j, core=1, zh=down))
    peers = 2 + core + 2 * number(x <= 2) + number(both(x <= 1, core == 1)) + 7 * number(owner)
    pl.semaphore_wait(bar, peers)

    def slot(kind, s):
        return kv_ref.at[kind, pl.ds(s * TOK, TOK), :]

    def rs(kind, s):
        return rsem.at[kind, s - 1]

    sends = Sends(ssem)
    for j in range(4):
        for t in range(2):
            mine = both(x == j, core == t)
            piece = own[t].at[:, pl.ds(j * HD, HD)]
            sends.start(both(owner, jnp.logical_not(mine)), piece, rel.at[blk], relsem.at[blk], p.at(x=j, core=t))
            local = pltpu.make_async_copy(piece, rel.at[blk], relsem.at[blk])
            pl.when(both(owner, mine))(local.start)
    for kind in range(2):
        pltpu.make_async_copy(own[kind], slot(kind, 0), lsem.at[kind]).start()
    for kind in range(2):
        s = 2 + kind - core
        sends.start(x <= 2, own[kind], slot(kind, s), rs(kind, s), p.at(x=x + 1, core=kind))
    for kind in range(2):
        sends.start(both(x <= 1, core == 1), own[kind], slot(kind, 3), rs(kind, 3), p.at(x=x + 2, core=0))
    for kind in range(2):
        sends.start(core == 0, own[kind], slot(kind, 1), rs(kind, 1), p.at(core=1))
    lanes = pl.ds(pl.multiple_of(x * HD, HD), HD)

    def part(s):
        return kv_ref.at[core, pl.ds(s * TOK, TOK), lanes]

    for b in range(3):
        arrived(rel.at[b], relsem.at[b])
        s = (3 - b) + (0 if b == 0 else core)
        target = p.at(x=0, zh=up, core=0 if b == 0 else core)
        sends.start(None, rel.at[b], part(s), rsem.at[core, s - 1], target)
    for s in (1, 2):
        pl.when(core == 0)(lambda s=s: arrived(slot(0, s), rs(0, s)))
        pl.when(core == 1)(lambda s=s: arrived(slot(1, s + 1), rs(1, s + 1)))
        sends.start(core == 0, slot(0, s), slot(0, s + 1), rs(0, s + 1), p.at(core=1))
        sends.start(core == 1, slot(1, s + 1), slot(1, s), rs(1, s), p.at(core=0))
        if s == 1:
            sends.start(both(x == 0, core == 0), slot(0, 1), slot(0, 3), rs(0, 3), p.at(x=1, core=0))
            sends.start(both(x == 0, core == 1), slot(1, 2), slot(1, 3), rs(1, 3), p.at(x=1, core=0))

    @pl.when(core == 0)
    def _():
        arrived(slot(0, 3), rs(0, 3))
        for s in (1, 2, 3):
            arrived(slot(1, s), rs(1, s))

    @pl.when(core == 1)
    def _():
        arrived(slot(1, 1), rs(1, 1))
        for s in (1, 2, 3):
            arrived(slot(0, s), rs(0, s))

    for kind in range(2):
        pltpu.make_async_copy(own[kind], slot(kind, 0), lsem.at[kind]).wait()
    sends.finish()


def gather(keys, values):
    return pl.pallas_call(
        gather_kernel,
        out_shape=jax.ShapeDtypeStruct((2, STEPS * TOK, KVH * HD), BF),
        in_specs=[pl.BlockSpec(memory_space=pl.ANY)] * 2,
        out_specs=pl.BlockSpec(memory_space=pl.ANY),
        scratch_shapes=[
            pltpu.VMEM((3, TOK, HD), BF),
            pltpu.SemaphoreType.DMA((24,)),
            pltpu.SemaphoreType.DMA((2, 3)),
            pltpu.SemaphoreType.DMA((3,)),
            pltpu.SemaphoreType.DMA((2,)),
        ],
        compiler_params=pltpu.CompilerParams(collective_id=0, has_side_effects=True),
    )(keys, values)


def attend_kernel(order_ref, q_ref, do_ref, k_ref, v_ref, o_ref, dq_ref, dkv_ref, gram_ref, bias, kt, vt, dk, dv):
    p = pl.program_id(0)
    c = lax.axis_index("ctx")
    half = TOK // 2

    @pl.when(p == 0)
    def _():
        row = lax.broadcasted_iota(jnp.int32, (half, TOK), 0)
        col = lax.broadcasted_iota(jnp.int32, (half, TOK), 1)
        qa, qb = order_ref[2 * c], order_ref[2 * c + 1]
        query_place = jnp.where(col < half, qa * half + col, qb * half + (col - half))
        for s in range(STEPS):
            kc = (c - s + 32) % 32
            for part in range(2):
                key_place = order_ref[2 * kc + part] * half + row
                b = jnp.where(key_place <= query_place, 0.0, NEG).astype(F32)
                rows = pl.ds(s * TOK + part * half, half)
                bias[rows, 0:TOK] = b
                bias[rows, TOK:2 * TOK] = b

    @pl.when(p % 4 == 0)
    def _():
        kt[...] = jnp.transpose(k_ref[0])
        vt[...] = jnp.transpose(v_ref[0])
        dk[...] = jnp.zeros_like(dk)
        dv[...] = jnp.zeros_like(dv)

    q2 = jnp.concatenate([q_ref[:, 0:HD], q_ref[:, HD:2 * HD]], axis=0)
    do2 = jnp.concatenate([do_ref[:, 0:HD], do_ref[:, HD:2 * HD]], axis=0)
    s = dot(k_ref[0], q2, 1, 1) * (SCALE * LOG2E) + bias[...]
    dp = dot(v_ref[0], do2, 1, 1)
    m = jnp.max(s, axis=0, keepdims=True)
    w = jnp.exp2(s - m)
    total = jnp.sum(w, axis=0, keepdims=True)
    mixed = jnp.sum(w * dp, axis=0, keepdims=True)
    inv = 1.0 / total
    delta = mixed * inv
    prob = w * inv
    pb = prob.astype(BF)
    ds = (prob * (dp - delta)).astype(BF)
    ot = dot(vt[...], pb, 1, 0).astype(BF)
    dqt = (dot(kt[...], ds, 1, 0) * SCALE).astype(BF)
    for h in range(2):
        lanes = slice(h * HD, (h + 1) * HD)
        oh = ot[:, h * TOK:(h + 1) * TOK]
        o_ref[:, lanes] = jnp.transpose(oh)
        dq_ref[:, lanes] = jnp.transpose(dqt[:, h * TOK:(h + 1) * TOK])
        gram_ref[h, 0] = dot(oh, oh, 1, 1).astype(BF)
    dv[...] += dot(pb, do2, 1, 0)
    dk[...] += dot(ds, q2, 1, 0)

    @pl.when(p % 4 == 3)
    def _():
        dkv_ref[0] = (dk[...] * SCALE).astype(BF)
        dkv_ref[1] = dv[...].astype(BF)


def attend(order, q, do, kv):
    heads = q.shape[1] // HD
    keys = STEPS * TOK
    return pl.pallas_call(
        attend_kernel,
        grid=(heads // 2,),
        in_specs=[
            pl.BlockSpec(memory_space=pltpu.SMEM),
            pl.BlockSpec((TOK, 2 * HD), lambda p: (0, p)),
            pl.BlockSpec((TOK, 2 * HD), lambda p: (0, p)),
            pl.BlockSpec((1, keys, HD), lambda p: (0, 0, p // 4)),
            pl.BlockSpec((1, keys, HD), lambda p: (1, 0, p // 4)),
        ],
        out_specs=[
            pl.BlockSpec((TOK, 2 * HD), lambda p: (0, p)),
            pl.BlockSpec((TOK, 2 * HD), lambda p: (0, p)),
            pl.BlockSpec((2, keys, HD), lambda p: (0, 0, p // 4)),
            pl.BlockSpec((2, 1, HD, HD), lambda p: (0, p, 0, 0)),
        ],
        out_shape=[
            jax.ShapeDtypeStruct((TOK, heads * HD), BF),
            jax.ShapeDtypeStruct((TOK, heads * HD), BF),
            jax.ShapeDtypeStruct((2, keys, KVH * HD), BF),
            jax.ShapeDtypeStruct((2, heads // 2, HD, HD), BF),
        ],
        scratch_shapes=[
            pltpu.VMEM((keys, 2 * TOK), F32),
            pltpu.VMEM((HD, keys), BF),
            pltpu.VMEM((HD, keys), BF),
            pltpu.VMEM((keys, HD), F32),
            pltpu.VMEM((keys, HD), F32),
        ],
        compiler_params=pltpu.CompilerParams(vmem_limit_bytes=32 * 2**20),
    )(order, q, do, kv, kv)


def reduce_kernel(
    dkv_ref, gram_ref, dk_ref, dv_ref, of_ref, gf_ref,
    mate, snd, rel, in1, in2,
    g0, ay, ry, ax, rx, az, rz, ah, rh,
    zown, zin, cs, cr, xs, xr, ls, lr, fs, fr,
    ssem, msem, relsem, in1sem, in2sem, osem, gsem, lsem,
):
    p = Place()
    x, core, y, zl, zh = p.x, p.core, p.y, p.zl, p.zh
    down = (zh + 3) % 4
    up = (zh + 1) % 4
    other = 1 - core
    bar = pltpu.get_barrier_semaphore()

    def ring(v, j):
        return (v + j) % 4

    for j in range(4):
        for t in range(2):
            signal(jnp.logical_not(both(x == j, core == t)), bar, p.at(x=j, core=t))
    for j in (1, 2, 3):
        signal(None, bar, p.at(y=ring(y, j)))
        signal(None, bar, p.at(zl=ring(zl, j)))
        signal(None, bar, p.at(zh=ring(zh, j)))
    for j in range(4):
        for t in range(2):
            signal(x == 3, bar, p.at(x=j, core=t, zh=up))
            signal(both(x == 2, core == 1), bar, p.at(x=j, core=t, zh=up))
        signal(jnp.logical_not(both(y == zh, zh == j)), bar, p.at(y=zh, zh=j))
    pl.semaphore_wait(bar, 7 + 9 + 3 + 4 - number(y == zh))

    sends = Sends(ssem)
    part = lambda kind, s: dkv_ref.at[kind, pl.ds(s * TOK, TOK), :]

    for i in range(2):
        sends.start(core == 0, part(1, 1 + i), mate.at[i], msem.at[i], p.at(core=1))
        sends.start(core == 1, part(0, 2 + i), mate.at[i], msem.at[i], p.at(core=0))
    for kind in range(2):
        sends.start(core == 1, part(kind, 1), in2.at[kind], in2sem.at[kind], p.at(core=0))
        sends.start(both(core == 0, x >= 2), part(kind, 3), in2.at[kind], in2sem.at[kind], p.at(x=x - 2, core=1))
        for j in range(4):
            piece = dkv_ref.at[kind, pl.ds(3 * TOK, TOK), pl.ds(j * HD, HD)]
            for sx, b in ((0, 2), (1, 3)):
                here = both(core == 0, x == sx)
                if kind == 0 and j == sx:
                    pl.when(here)(pltpu.make_async_copy(piece, rel.at[b], relsem.at[b]).start)
                else:
                    sends.start(here, piece, rel.at[b], relsem.at[b], p.at(x=j, core=kind))
    sends.start(None, gram_ref.at[other], g0, osem.at[0], p.at(core=other))

    for i in range(2):
        arrived(mate.at[i], msem.at[i])
        mine = dkv_ref[core, pl.ds(pl.multiple_of((1 + i + core) * TOK, TOK), TOK), :]
        snd[i] = (mine.astype(F32) + mate[i].astype(F32)).astype(BF)
        sends.start(x >= 1, snd.at[i], in1.at[core], in1sem.at[core], p.at(x=x - 1, core=1 - i))
        for j in range(4):
            piece = snd.at[i, :, pl.ds(j * HD, HD)]
            if j == 0:
                pl.when(x == 0)(pltpu.make_async_copy(piece, rel.at[i], relsem.at[i]).start)
            else:
                sends.start(x == 0, piece, rel.at[i], relsem.at[i], p.at(x=j))
    lanes = pl.ds(pl.multiple_of(x * HD, HD), HD)
    arrived(rel.at[2], relsem.at[2])
    sends.start(None, rel.at[2], in2.at[core, :, lanes], in2sem.at[core], p.at(x=2, core=1, zh=down))
    arrived(rel.at[1], relsem.at[1])
    sends.start(None, rel.at[1], in1.at[core, :, lanes], in1sem.at[core], p.at(x=3, core=0, zh=down))
    arrived(rel.at[0], relsem.at[0])
    arrived(rel.at[3], relsem.at[3])
    rel[4] = (rel[0].astype(F32) + rel[3].astype(F32)).astype(BF)
    sends.start(None, rel.at[4], in1.at[core, :, lanes], in1sem.at[core], p.at(x=3, core=1, zh=down))

    arrived(g0, osem.at[0])

    def rows_of_y(h, _):
        both_cores = gram_ref[core, h].astype(F32) + g0[h].astype(F32)
        split = both_cores.reshape(4, 4, 8, HD)
        for j in range(4):
            ay[j, pl.ds(pl.multiple_of(h * 32, 32), 32), :] = split[:, j].reshape(32, HD).astype(BF)
        return 0

    lax.fori_loop(0, 16, rows_of_y, 0)
    for j in (1, 2, 3):
        sends.start(None, ay.at[ring(y, j)], ry.at[j - 1], osem.at[j], p.at(y=ring(y, j)))
    for j in (1, 2, 3):
        arrived(ry.at[j - 1], osem.at[j])

    def heads_of_x(h, _):
        rows = pl.ds(pl.multiple_of(h * 32, 32), 32)
        total = ay[y, rows, :].astype(F32)
        for j in range(3):
            total = total + ry[j, rows, :].astype(F32)
        ax[h % 4, pl.ds(pl.multiple_of((h // 4) * 32, 32), 32), :] = total.astype(BF)
        return 0

    lax.fori_loop(0, 16, heads_of_x, 0)
    for j in (1, 2, 3):
        sends.start(None, ax.at[ring(x, j)], rx.at[j - 1], osem.at[3 + j], p.at(x=ring(x, j)))
    for j in (1, 2, 3):
        arrived(rx.at[j - 1], osem.at[3 + j])
    total = ax[x].astype(F32)
    for j in range(3):
        total = total + rx[j].astype(F32)
    total = total.reshape(4, 4, 8, HD)
    for j in range(4):
        az[j] = total[:, j]
    for j in (1, 2, 3):
        sends.start(None, az.at[ring(zl, j)], rz.at[j - 1], osem.at[6 + j], p.at(zl=ring(zl, j)))
    for j in (1, 2, 3):
        arrived(rz.at[j - 1], osem.at[6 + j])
    ah[...] = az[zl] + rz[0] + rz[1] + rz[2]
    for j in (1, 2, 3):
        sends.start(None, ah.at[ring(zh, j)], rh.at[j - 1], osem.at[9 + j], p.at(zh=ring(zh, j)))

    for kind in range(2):
        arrived(in1.at[kind], in1sem.at[kind])
    last = both(x == 3, core == 1)
    outs = (dk_ref, dv_ref)
    for kind in range(2):
        near = dkv_ref[kind, pl.ds(0, TOK), :].astype(F32) + in1[kind].astype(F32)

        @pl.when(last)
        def _():
            outs[kind][0] = near.astype(BF)

        @pl.when(jnp.logical_not(last))
        def _():
            arrived(in2.at[kind], in2sem.at[kind])
            outs[kind][0] = (near + in2[kind].astype(F32)).astype(BF)

    for g in range(KVH):
        for kind in range(2):
            zown[g, :, pl.ds(kind * HD, HD)] = outs[kind][0, :, pl.ds(g * HD, HD)]
    for j in (1, 2, 3):
        sends.start(None, zown.at[ring(y, j)], zin.at[j - 1], gsem.at[j - 1], p.at(y=ring(y, j)))
    gram = dot(zown[y], zown[y], 0, 0)
    for j in (1, 2, 3):
        arrived(zin.at[j - 1], gsem.at[j - 1])
        z = zin[j - 1]
        gram = gram + dot(z, z, 0, 0)
    gram = gram.reshape(4, 2, 32, 2 * HD)
    for c2 in range(2):
        cs[c2] = gram[:, c2].astype(BF)
    sends.start(None, cs.at[other], cr, gsem.at[3], p.at(core=other))
    arrived(cr, gsem.at[3])
    xs[...] = (cs[core].astype(F32) + cr[...].astype(F32)).astype(BF)
    for j in (1, 2, 3):
        sends.start(None, xs.at[ring(x, j)], xr.at[j - 1], gsem.at[3 + j], p.at(x=ring(x, j)))
    total = xs[x].astype(F32)
    for j in (1, 2, 3):
        arrived(xr.at[j - 1], gsem.at[3 + j])
        total = total + xr[j - 1].astype(F32)
    ls[...] = total.reshape(4, 8, 2 * HD)
    for j in (1, 2, 3):
        sends.start(None, ls.at[ring(zl, j)], lr.at[j - 1], gsem.at[6 + j], p.at(zl=ring(zl, j)))
    total = ls[zl]
    for j in (1, 2, 3):
        arrived(lr.at[j - 1], gsem.at[6 + j])
        total = total + lr[j - 1]
    for j in range(4):
        fs[j] = total[2 * j:2 * j + 2, :]
    for j in range(4):
        away = jnp.logical_not(both(y == j, zh == y))
        sends.start(away, fs.at[j], fr.at[zh], gsem.at[10 + zh], p.at(y=j, zh=y))
        pl.when(both(y == j, zh == y))(
            pltpu.make_async_copy(fs.at[j], fr.at[zh], gsem.at[10 + zh]).start)
    tokens = float(512 * TOK)
    for j in (1, 2, 3):
        arrived(rh.at[j - 1], osem.at[9 + j])
    of_ref[...] = (ah[zh] + rh[0] + rh[1] + rh[2]) / tokens
    for j in range(4):
        arrived(fr.at[j], gsem.at[10 + j])
    gf_ref[...] = (fr[0] + fr[1] + fr[2] + fr[3]) / tokens
    sends.finish()


def reduce(dkv, gram):
    vmem = pl.BlockSpec(memory_space=pltpu.VMEM)
    wide = KVH * HD
    return pl.pallas_call(
        reduce_kernel,
        out_shape=[
            jax.ShapeDtypeStruct((1, TOK, wide), BF),
            jax.ShapeDtypeStruct((1, TOK, wide), BF),
            jax.ShapeDtypeStruct((8, HD), F32),
            jax.ShapeDtypeStruct((2, 2 * HD), F32),
        ],
        in_specs=[vmem, vmem],
        out_specs=[vmem] * 4,
        scratch_shapes=[
            pltpu.VMEM((2, TOK, wide), BF),
            pltpu.VMEM((2, TOK, wide), BF),
            pltpu.VMEM((5, TOK, HD), BF),
            pltpu.VMEM((2, TOK, wide), BF),
            pltpu.VMEM((2, TOK, wide), BF),
            pltpu.VMEM((16, HD, HD), BF),
            pltpu.VMEM((4, 512, HD), BF),
            pltpu.VMEM((3, 512, HD), BF),
            pltpu.VMEM((4, 128, HD), BF),
            pltpu.VMEM((3, 128, HD), BF),
            pltpu.VMEM((4, 4, 8, HD), F32),
            pltpu.VMEM((3, 4, 8, HD), F32),
            pltpu.VMEM((4, 8, HD), F32),
            pltpu.VMEM((3, 8, HD), F32),
            pltpu.VMEM((4, TOK, 2 * HD), BF),
            pltpu.VMEM((3, TOK, 2 * HD), BF),
            pltpu.VMEM((2, 4, 32, 2 * HD), BF),
            pltpu.VMEM((4, 32, 2 * HD), BF),
            pltpu.VMEM((4, 32, 2 * HD), BF),
            pltpu.VMEM((3, 32, 2 * HD), BF),
            pltpu.VMEM((4, 8, 2 * HD), F32),
            pltpu.VMEM((3, 8, 2 * HD), F32),
            pltpu.VMEM((4, 2, 2 * HD), F32),
            pltpu.VMEM((4, 2, 2 * HD), F32),
            pltpu.SemaphoreType.DMA((72,)),
            pltpu.SemaphoreType.DMA((2,)),
            pltpu.SemaphoreType.DMA((4,)),
            pltpu.SemaphoreType.DMA((2,)),
            pltpu.SemaphoreType.DMA((2,)),
            pltpu.SemaphoreType.DMA((13,)),
            pltpu.SemaphoreType.DMA((14,)),
            pltpu.SemaphoreType.DMA((2,)),
        ],
        compiler_params=pltpu.CompilerParams(
            collective_id=1, has_side_effects=True, vmem_limit_bytes=32 * 2**20),
    )(dkv, gram)


def local(queries, key_heads, value_heads, out_grad, block_order):
    kv = gather(key_heads[0], value_heads[0])
    attn, dq, dkv, gram = attend(block_order, queries[0], out_grad[0], kv)
    dk, dv, out_factor, grad_factor = reduce(dkv, gram)
    return attn[None], dq[None], dk, dv, out_factor, grad_factor


def solution(mesh):
    rows = P("dp", "ctx", None)
    return jax.shard_map(
        local,
        mesh=mesh,
        in_specs=(rows, rows, rows, rows, P()),
        out_specs=(rows, rows, rows, rows, P(("ctx", "dp"), None), P(("ctx", "dp"), None)),
        check_vma=False,
    )
```

```python
import math

import jax
import jax.numpy as jnp
from jax import lax
from jax.experimental import pallas as pl
from jax.experimental.pallas import tpu as pltpu
from jax.sharding import PartitionSpec as P

HD = 128
STEPS = 4
TOK = 128
QUARTER = TOK // 4
KVH = 4
NEG = -1e30
LOG2E = 1.0 / math.log(2.0)
SCALE = 1.0 / math.sqrt(HD)
MESH = pl.DeviceIdType.MESH
BF = jnp.bfloat16
F32 = jnp.float32


def dot(a, b, ca, cb):
    return lax.dot_general(a, b, (((ca,), (cb,)), ((), ())), preferred_element_type=F32)


class Place:
    def __init__(self):
        c, d = lax.axis_index("ctx"), lax.axis_index("dp")
        self.zh, self.x, self.core = c // 8, (c % 8) // 2, c % 2
        self.zl, self.y = d // 4, d % 4

    def at(self, x=None, core=None, y=None, zl=None, zh=None):
        x = self.x if x is None else x
        core = self.core if core is None else core
        y = self.y if y is None else y
        zl = self.zl if zl is None else zl
        zh = self.zh if zh is None else zh
        return (zh * 8 + x * 2 + core, zl * 4 + y)


def both(*conds):
    total = conds[0]
    for cond in conds[1:]:
        total = jnp.logical_and(total, cond)
    return total


class Sends:
    def __init__(self, sems):
        self.sems, self.keys = sems, {}

    def start(self, key, cond, src, dst, recv_sem, device, whole):
        if key not in self.keys:
            self.keys[key] = (len(self.keys), cond, whole)
        copy = pltpu.make_async_remote_copy(
            src_ref=src, dst_ref=dst, send_sem=self.sems.at[self.keys[key][0]], recv_sem=recv_sem,
            device_id=device, device_id_type=MESH,
        )
        if cond is None:
            copy.start()
        else:
            pl.when(cond)(copy.start)

    def finish(self):
        for index, cond, whole in self.keys.values():
            def act(index=index, whole=whole):
                arrived(whole, self.sems.at[index])
            if cond is None:
                act()
            else:
                pl.when(cond)(act)


def arrived(dst, sem):
    pltpu.make_async_copy(dst, dst, sem).wait()


def local_copy(cond, src, dst, sem):
    copy = pltpu.make_async_copy(src, dst, sem)
    if cond is None:
        copy.start()
    else:
        pl.when(cond)(copy.start)


def signal(cond, sem, device):
    def act():
        pl.semaphore_signal(sem, inc=1, device_id=device, device_id_type=MESH)
    if cond is None:
        act()
    else:
        pl.when(cond)(act)


def number(cond):
    return jnp.where(cond, 1, 0).astype(jnp.int32)


def lanes_of(g, count=1):
    if isinstance(g, int):
        return pl.ds(g * HD, count * HD)
    return pl.ds(pl.multiple_of(g * HD, HD), count * HD)


def rows_of(j):
    return pl.ds(pl.multiple_of(j * QUARTER, QUARTER), QUARTER)


def ring(v, j):
    return (v + j) % 4


def fused_kernel(
    order_ref, q_hbm, do_hbm, k_hbm, v_hbm,
    attn_hbm, dq_hbm, dk_ref, dv_ref, of_ref, gf_ref,
    qv, dov, ov, dqv, kvs, dkv, gram, bias,
    rel, mate, snd, rel2, relsum, in1, in2,
    g0, ay, ry, ax, rx, az, rz, ah, rh,
    zown, zin, cs, cr, xs, xr, ls, lr, fs, fr,
    ssem, qsem, outsem, ownsem, rsem, relsem, msem, rel2sem, in1sem, in2sem,
    o0sem, oysem, oxsem, ozsem, gsem, ready2, ready3,
):
    p = Place()
    x, core, y, zl, zh = p.x, p.core, p.y, p.zl, p.zh
    up, down, other = ring(zh, 1), ring(zh, 3), 1 - core
    own = (k_hbm, v_hbm)
    owner = jnp.logical_or(x == 3, both(x == 2, core == 1))
    blk = 2 * (x - 2) + core - 1
    bar = pltpu.get_barrier_semaphore()
    sends = Sends(ssem)

    core0, core1 = core == 0, core == 1
    x0, x_up, x0core0, x0core1 = x == 0, x >= 1, both(x == 0, core == 0), both(x == 0, core == 1)
    tail_at = {0: x0core0, 1: both(x == 1, core == 0)}
    two_up = both(core == 0, x >= 2)
    elsewhere = [y != g for g in range(KVH)]
    tall, thin, one_slot = mate.at[0], rel2.at[0], kvs.at[0, :, pl.ds(0, TOK), :]
    one_ay, one_ax, one_z = ay.at[0], ax.at[0], zown.at[0]

    signal(None, bar, p.at(zh=up))
    signal(None, bar, p.at(zh=down))
    for j in range(4):
        signal(x == 0, bar, p.at(x=j, zh=down))
        signal(both(x == 0, core == 0), bar, p.at(x=j, core=1, zh=down))
        for t in range(2):
            signal(x == 3, bar, p.at(x=j, core=t, zh=up))
            signal(both(x == 2, core == 1), bar, p.at(x=j, core=t, zh=up))
    for j in (1, 2, 3):
        signal(None, bar, p.at(zl=ring(zl, j)))
        signal(None, bar, p.at(y=ring(y, j)))
    for j in range(4):
        for t in range(2):
            signal(jnp.logical_not(both(x == j, core == t)), bar, p.at(x=j, core=t))

    for g in range(KVH):
        heads = lanes_of(8 * g, 8)
        local_copy(None, q_hbm.at[:, heads], qv.at[:, heads], qsem.at[0, g])
        local_copy(None, do_hbm.at[:, heads], dov.at[:, heads], qsem.at[1, g])
        if g == 0:
            for kind in range(2):
                for i in range(KVH):
                    local_copy(None, own[kind].at[:, lanes_of(i)], kvs.at[kind, i, pl.ds(0, TOK), :], ownsem.at[kind])
    half = TOK // 2
    c = lax.axis_index("ctx")
    row = lax.broadcasted_iota(jnp.int32, (half, TOK), 0)
    col = lax.broadcasted_iota(jnp.int32, (half, TOK), 1)
    query_place = jnp.where(col < half, order_ref[2 * c] * half + col, order_ref[2 * c + 1] * half + (col - half))
    for s in range(STEPS):
        kc = (c - s + 32) % 32
        for part in range(2):
            key_place = order_ref[2 * kc + part] * half + row
            bias[pl.ds(s * TOK + part * half, half), :] = jnp.where(key_place <= query_place, 0.0, NEG).astype(F32)
    pl.semaphore_wait(bar, 7 + 3 + 3 + 2 + 1 + core + 3)

    def slot(kind, s, g):
        return kvs.at[kind, g, pl.ds(s * TOK, TOK), :]

    for kind in range(2):
        arrived(kvs.at[kind, :, pl.ds(0, TOK), :], ownsem.at[kind])

    for wide in range(2):
        group = pl.ds(0, 1) if wide == 0 else pl.ds(1, 3)
        for j in range(4):
            for t in range(2):
                mine = both(x == j, core == t)
                piece = kvs.at[t, group, pl.ds(j * QUARTER, QUARTER), :]
                target = rel.at[blk, group]
                sends.start(("spread", j, t), both(owner, jnp.logical_not(mine)), piece, target,
                            relsem.at[blk, wide], p.at(x=j, core=t), rel.at[0])
                local_copy(both(owner, mine), piece, target, relsem.at[blk, wide])
    for g in range(KVH):
        for kind in range(2):
            piece = slot(kind, 0, g)
            s = 2 + kind - core
            sends.start(("near", kind), x <= 2, piece, slot(kind, s, g), rsem.at[kind, s - 1, g],
                        p.at(x=x + 1, core=kind), one_slot)
            sends.start(("far", kind), both(x <= 1, core == 1), piece, slot(kind, 3, g), rsem.at[kind, 2, g],
                        p.at(x=x + 2, core=0), one_slot)
            sends.start(("own", kind), core == 0, piece, slot(kind, 1, g), rsem.at[kind, 0, g],
                        p.at(core=1), one_slot)
        if g == 0:
            relay_in(rel, relsem, 0)
            relay_out(sends, p, rel, kvs, rsem, 0, up)
    relay_in(rel, relsem, 1)
    for g in range(1, KVH):
        relay_out(sends, p, rel, kvs, rsem, g, up)
    for side in (up, down):
        signal(None, ready2, p.at(zh=side))

    def forward(g):
        for s in (1, 2):
            pl.when(core == 0)(lambda: arrived(slot(0, s, g), rsem.at[0, s - 1, g]))
            pl.when(core == 1)(lambda: arrived(slot(1, s + 1, g), rsem.at[1, s, g]))
            sends.start(("fk", s), core0, slot(0, s, g), slot(0, s + 1, g), rsem.at[0, s, g],
                        p.at(core=1), one_slot)
            sends.start(("fv", s), core1, slot(1, s + 1, g), slot(1, s, g), rsem.at[1, s - 1, g],
                        p.at(core=0), one_slot)
            if s == 1:
                sends.start(("f3k",), x0core0, slot(0, 1, g), slot(0, 3, g), rsem.at[0, 2, g],
                            p.at(x=1, core=0), one_slot)
                sends.start(("f3v",), x0core1, slot(1, 2, g), slot(1, 3, g), rsem.at[1, 2, g],
                            p.at(x=1, core=0), one_slot)

    def slots_ready(g):
        @pl.when(core == 0)
        def _():
            arrived(slot(0, 3, g), rsem.at[0, 2, g])
            for s in (1, 2, 3):
                arrived(slot(1, s, g), rsem.at[1, s - 1, g])

        @pl.when(core == 1)
        def _():
            arrived(slot(1, 1, g), rsem.at[1, 0, g])
            for s in (1, 2, 3):
                arrived(slot(0, s, g), rsem.at[0, s - 1, g])

    def compute(g):
        keys = kvs[0, g]
        values = kvs[1, g]
        q_all = jnp.concatenate([qv[:, lanes_of(8 * g + h)] for h in range(8)], axis=0)
        do_all = jnp.concatenate([dov[:, lanes_of(8 * g + h)] for h in range(8)], axis=0)
        mask = jnp.concatenate([bias[...], bias[...]], axis=1)
        probs, dscores = [], []
        for pair in range(4):
            cut = slice(pair * 2 * TOK, (pair + 1) * 2 * TOK)
            s = dot(keys, q_all[cut], 1, 1) * (SCALE * LOG2E) + mask
            dp = dot(values, do_all[cut], 1, 1)
            m = jnp.max(s, axis=0, keepdims=True)
            w = jnp.exp2(s - m)
            total = jnp.sum(w, axis=0, keepdims=True)
            mixed = jnp.sum(w * dp, axis=0, keepdims=True)
            inv = 1.0 / total
            delta = mixed * inv
            prob = w * inv
            probs.append(prob.astype(BF))
            dscores.append((prob * (dp - delta)).astype(BF))
        pb = jnp.concatenate(probs, axis=1)
        ds = jnp.concatenate(dscores, axis=1)
        dkv[1, g] = dot(pb, do_all, 1, 0).astype(BF)
        dkv[0, g] = (dot(ds, q_all, 1, 0) * SCALE).astype(BF)
        ot = dot(jnp.transpose(values), pb, 1, 0).astype(BF)
        dqt = (dot(jnp.transpose(keys), ds, 1, 0) * SCALE).astype(BF)
        for h in range(8):
            oh = ot[:, h * TOK:(h + 1) * TOK]
            ov[:, lanes_of(8 * g + h)] = jnp.transpose(oh)
            dqv[:, lanes_of(8 * g + h)] = jnp.transpose(dqt[:, h * TOK:(h + 1) * TOK])
            gram[h % 2, 4 * g + h // 2] = dot(oh, oh, 1, 1).astype(BF)
        heads = lanes_of(8 * g, 8)
        local_copy(None, ov.at[:, heads], attn_hbm.at[:, heads], outsem.at[0])
        local_copy(None, dqv.at[:, heads], dq_hbm.at[:, heads], outsem.at[1])

    def part(kind, s, g):
        return dkv.at[kind, g, pl.ds(s * TOK, TOK), :]

    def home1(g):
        for i in range(2):
            sends.start(("mv", i), core0, part(1, 1 + i, g), mate.at[i, g], msem.at[i, g], p.at(core=1), tall)
            sends.start(("mk", i), core1, part(0, 2 + i, g), mate.at[i, g], msem.at[i, g], p.at(core=0), tall)
        for kind in range(2):
            for j in range(4):
                piece = dkv.at[kind, g, pl.ds(3 * TOK + j * QUARTER, QUARTER), :]
                for sx, b in ((0, 2), (1, 3)):
                    here = tail_at[sx]
                    if kind == 0 and j == sx:
                        local_copy(here, piece, rel2.at[b, g], rel2sem.at[b, g])
                    else:
                        sends.start(("r3", kind, j, b), here, piece, rel2.at[b, g], rel2sem.at[b, g],
                                    p.at(x=j, core=kind), thin)
            sends.start(("m1", kind), core1, part(kind, 1, g), in2.at[kind, g], in2sem.at[kind, g], p.at(core=0), tall)
            sends.start(("m3", kind), two_up, part(kind, 3, g), in2.at[kind, g],
                        in2sem.at[kind, g], p.at(x=x - 2, core=1), tall)

    def home2(g):
        for i in range(2):
            arrived(mate.at[i, g], msem.at[i, g])
            rows = pl.ds(pl.multiple_of((1 + i + core) * TOK, TOK), TOK)
            mine = dkv[core, g, rows, :]
            snd[i, g] = (mine.astype(F32) + mate[i, g].astype(F32)).astype(BF)
            sends.start(("n", i), x_up, snd.at[i, g], in1.at[core, g], in1sem.at[core, g],
                        p.at(x=x - 1, core=1 - i), tall)
            for j in range(4):
                piece = snd.at[i, g, pl.ds(j * QUARTER, QUARTER), :]
                if j == 0:
                    local_copy(x0, piece, rel2.at[i, g], rel2sem.at[i, g])
                else:
                    sends.start(("r", i, j), x0, piece, rel2.at[i, g], rel2sem.at[i, g], p.at(x=j), thin)

    def home3(g):
        def there(ref):
            return ref.at[core, g, rows_of(x), :]

        arrived(rel2.at[2, g], rel2sem.at[2, g])
        sends.start(("h2",), None, rel2.at[2, g], there(in2), in2sem.at[core, g], p.at(x=2, core=1, zh=down), thin)
        arrived(rel2.at[1, g], rel2sem.at[1, g])
        sends.start(("h1",), None, rel2.at[1, g], there(in1), in1sem.at[core, g], p.at(x=3, core=0, zh=down), thin)
        arrived(rel2.at[0, g], rel2sem.at[0, g])
        arrived(rel2.at[3, g], rel2sem.at[3, g])
        relsum[g] = (
            rel2[0, g].astype(F32) + rel2[3, g].astype(F32)).astype(BF)
        sends.start(("h0",), None, relsum.at[g], there(in1), in1sem.at[core, g], p.at(x=3, core=1, zh=down), thin)

    last = both(x == 3, core == 1)
    outs = (dk_ref, dv_ref)

    def home4(g):
        for kind in range(2):
            arrived(in1.at[kind, g], in1sem.at[kind, g])
            near = dkv[kind, g, pl.ds(0, TOK), :].astype(F32) + in1[kind, g].astype(F32)

            @pl.when(last)
            def _():
                outs[kind][0, :, lanes_of(g)] = near.astype(BF)

            @pl.when(jnp.logical_not(last))
            def _():
                arrived(in2.at[kind, g], in2sem.at[kind, g])
                outs[kind][0, :, lanes_of(g)] = (near + in2[kind, g].astype(F32)).astype(BF)

            zown[g, :, pl.ds(kind * HD, HD)] = outs[kind][0, :, lanes_of(g)]
        at = ring(y, 7 - g)
        sends.start(("z", g), elsewhere[g], zown.at[g], zin.at[at], gsem.at[at], p.at(y=g), one_z)

    def out1(g):
        mine = pl.ds(4 * g, 4)
        sends.start(("oc",), None, gram.at[other, mine], g0.at[mine], o0sem.at[g], p.at(core=other), g0)

    def out2(g):
        arrived(g0.at[pl.ds(4 * g, 4)], o0sem.at[g])
        for h in range(4):
            pair_sum = gram[core, 4 * g + h].astype(F32) + g0[4 * g + h].astype(F32)
            split = pair_sum.reshape(4, 4, 8, HD)
            for j in range(4):
                ay[g, j, pl.ds(h * 32, 32), :] = split[:, j].reshape(32, HD).astype(BF)
        for j in (1, 2, 3):
            sends.start(("oy", j), None, ay.at[g, ring(y, j)], ry.at[g, j - 1], oysem.at[g, j - 1], p.at(y=ring(y, j)), one_ay)

    def out3(g):
        for j in range(3):
            arrived(ry.at[g, j], oysem.at[g, j])
        total = ay[g, y].astype(F32)
        for j in range(3):
            total = total + ry[g, j].astype(F32)
        ax[g] = total.reshape(4, 32, HD).astype(BF)
        for j in (1, 2, 3):
            sends.start(("ox", j), None, ax.at[g, ring(x, j)], rx.at[g, j - 1], oxsem.at[g, j - 1], p.at(x=ring(x, j)), one_ax)

    def out4(g):
        for j in range(3):
            arrived(rx.at[g, j], oxsem.at[g, j])
        total = ax[g, x].astype(F32)
        for j in range(3):
            total = total + rx[g, j].astype(F32)
        total = total.reshape(4, 8, HD)
        for j in range(4):
            az[j, g] = total[j]

    forward(0)

    def step(g, _):
        pl.when(g < 3)(lambda: forward(jnp.minimum(g + 1, 3)))
        slots_ready(g)
        heads = lanes_of(8 * g, 8)
        arrived(qv.at[:, heads], qsem.at[0, g])
        arrived(dov.at[:, heads], qsem.at[1, g])
        compute(g)
        home1(g)
        out1(g)

        @pl.when(g >= 1)
        def _():
            home2(g - 1)
            out2(g - 1)

        @pl.when(g >= 2)
        def _():
            home3(g - 2)
            out3(g - 2)

        @pl.when(g == 3)
        def _():
            home4(0)
            out4(0)
        return 0

    lax.fori_loop(0, KVH, step, 0)
    home2(3)
    home3(2)
    out2(3)
    out3(2)
    home4(1)
    out4(1)
    home3(3)
    out3(3)
    home4(2)
    out4(2)
    pl.semaphore_wait(ready2, 2)
    for j in (1, 2, 3):
        signal(None, ready3, p.at(y=ring(y, j)))
    out4(3)
    for j in (1, 2, 3):
        sends.start(("oz", j), None, az.at[ring(zl, j)], rz.at[j - 1], ozsem.at[j - 1], p.at(zl=ring(zl, j)), rz.at[0])
    home4(3)
    for j in range(3):
        arrived(rz.at[j], ozsem.at[j])
    ah[...] = az[zl] + rz[0] + rz[1] + rz[2]
    for j in (1, 2, 3):
        sends.start(("oh", j), None, ah.at[ring(zh, j)], rh.at[j - 1], ozsem.at[2 + j], p.at(zh=ring(zh, j)), rh.at[0])

    mine = zown[y]
    total = dot(mine, mine, 0, 0)
    for j in range(3):
        arrived(zin.at[j], gsem.at[j])
        z = zin[j]
        total = total + dot(z, z, 0, 0)
    total = total.reshape(4, 2, 32, 2 * HD)
    for c2 in range(2):
        cs[c2] = total[:, c2].astype(BF)
    sends.start(("gc",), None, cs.at[other], cr, gsem.at[3], p.at(core=other), cr)
    arrived(cr, gsem.at[3])
    xs[...] = (cs[core].astype(F32) + cr[...].astype(F32)).astype(BF)
    for j in (1, 2, 3):
        sends.start(("gx", j), None, xs.at[ring(x, j)], xr.at[j - 1], gsem.at[3 + j], p.at(x=ring(x, j)), xr.at[0])
    total = xs[x].astype(F32)
    for j in range(3):
        arrived(xr.at[j], gsem.at[4 + j])
        total = total + xr[j].astype(F32)
    ls[...] = total.reshape(4, 8, 2 * HD)
    for j in (1, 2, 3):
        sends.start(("gz", j), None, ls.at[ring(zl, j)], lr.at[j - 1], gsem.at[6 + j], p.at(zl=ring(zl, j)), lr.at[0])
    pl.semaphore_wait(ready3, 3)
    total = ls[zl]
    for j in range(3):
        arrived(lr.at[j], gsem.at[7 + j])
        total = total + lr[j]
    for j in range(4):
        fs[j] = total[2 * j:2 * j + 2, :]
    for j in range(4):
        mine = both(y == j, zh == y)
        sends.start(("gf", j), jnp.logical_not(mine), fs.at[j], fr.at[zh], gsem.at[10 + zh], p.at(y=j, zh=y), fr.at[0])
        local_copy(mine, fs.at[j], fr.at[zh], gsem.at[10 + zh])
    tokens = float(512 * TOK)
    for j in range(3):
        arrived(rh.at[j], ozsem.at[3 + j])
    of_ref[...] = (ah[zh] + rh[0] + rh[1] + rh[2]) / tokens
    arrived(attn_hbm, outsem.at[0])
    arrived(dq_hbm, outsem.at[1])
    sends.finish()
    for j in range(4):
        arrived(fr.at[j], gsem.at[10 + j])
    gf_ref[...] = (fr[0] + fr[1] + fr[2] + fr[3]) / tokens


def relay_in(rel, relsem, wide):
    group = pl.ds(0, 1) if wide == 0 else pl.ds(1, 3)
    for b in range(3):
        arrived(rel.at[b, group], relsem.at[b, wide])


def relay_out(sends, p, rel, kvs, rsem, g, up):
    for b in range(3):
        s = (3 - b) + (0 if b == 0 else p.core)
        rows = pl.ds(pl.multiple_of(s * TOK + p.x * QUARTER, QUARTER), QUARTER)
        sends.start(("relay", b), None, rel.at[b, g], kvs.at[p.core, g, rows, :],
                    rsem.at[p.core, s - 1, g], p.at(x=0, zh=up, core=0 if b == 0 else p.core), rel.at[0])


def fused(order, q, do, keys, values):
    vmem, hbm = pl.BlockSpec(memory_space=pltpu.VMEM), pl.BlockSpec(memory_space=pl.ANY)
    wide, all_lanes = KVH * HD, q.shape[1]
    V = pltpu.VMEM
    D = pltpu.SemaphoreType.DMA
    return pl.pallas_call(
        fused_kernel,
        out_shape=[
            jax.ShapeDtypeStruct((TOK, all_lanes), BF),
            jax.ShapeDtypeStruct((TOK, all_lanes), BF),
            jax.ShapeDtypeStruct((1, TOK, wide), BF),
            jax.ShapeDtypeStruct((1, TOK, wide), BF),
            jax.ShapeDtypeStruct((8, HD), F32),
            jax.ShapeDtypeStruct((2, 2 * HD), F32),
        ],
        in_specs=[pl.BlockSpec(memory_space=pltpu.SMEM)] + [hbm] * 4,
        out_specs=[hbm, hbm] + [vmem] * 4,
        scratch_shapes=[
            V((TOK, all_lanes), BF), V((TOK, all_lanes), BF), V((TOK, all_lanes), BF), V((TOK, all_lanes), BF),
            V((2, KVH, STEPS * TOK, HD), BF), V((2, KVH, STEPS * TOK, HD), BF),
            V((2, 16, HD, HD), BF), V((STEPS * TOK, TOK), F32),
            V((3, KVH, QUARTER, HD), BF), V((2, KVH, TOK, HD), BF), V((2, KVH, TOK, HD), BF),
            V((4, KVH, QUARTER, HD), BF), V((KVH, QUARTER, HD), BF), V((2, KVH, TOK, HD), BF), V((2, KVH, TOK, HD), BF),
            V((16, HD, HD), BF), V((4, 4, 128, HD), BF), V((4, 3, 128, HD), BF),
            V((4, 4, 32, HD), BF), V((4, 3, 32, HD), BF),
            V((4, 4, 8, HD), F32), V((3, 4, 8, HD), F32), V((4, 8, HD), F32), V((3, 8, HD), F32),
            V((4, TOK, 2 * HD), BF), V((3, TOK, 2 * HD), BF),
            V((2, 4, 32, 2 * HD), BF), V((4, 32, 2 * HD), BF), V((4, 32, 2 * HD), BF), V((3, 32, 2 * HD), BF),
            V((4, 8, 2 * HD), F32), V((3, 8, 2 * HD), F32), V((4, 2, 2 * HD), F32), V((4, 2, 2 * HD), F32),
            D((96,)), D((2, 4)), D((2,)), D((2,)), D((2, 3, 4)), D((3, 2)), D((2, 4)), D((4, 4)), D((2, 4)), D((2, 4)),
            D((4,)), D((4, 3)), D((4, 3)), D((6,)), D((14,)),
            pltpu.SemaphoreType.REGULAR, pltpu.SemaphoreType.REGULAR,
        ],
        compiler_params=pltpu.CompilerParams(
            collective_id=0, has_side_effects=True, vmem_limit_bytes=60 * 2**20),
    )(order, q, do, keys, values)


def local(queries, key_heads, value_heads, out_grad, block_order):
    outs = fused(block_order, queries[0], out_grad[0], key_heads[0], value_heads[0])
    attn, dq, dk, dv, out_factor, grad_factor = outs
    return attn[None], dq[None], dk, dv, out_factor, grad_factor


def solution(mesh):
    rows = P("dp", "ctx", None)
    return jax.shard_map(
        local,
        mesh=mesh,
        in_specs=(rows, rows, rows, rows, P()),
        out_specs=(rows, rows, rows, rows, P(("ctx", "dp"), None), P(("ctx", "dp"), None)),
        check_vma=False,
    )
```

```python
import math

import jax
import jax.numpy as jnp
from jax import lax
from jax.experimental import pallas as pl
from jax.experimental.pallas import tpu as pltpu
from jax.sharding import PartitionSpec as P

HD = 128
STEPS = 4
TOK = 128
QUARTER = TOK // 4
KVH = 4
NEG = -1e30
LOG2E = 1.0 / math.log(2.0)
SCALE = 1.0 / math.sqrt(HD)
MESH = pl.DeviceIdType.MESH
BF = jnp.bfloat16
F32 = jnp.float32


def dot(a, b, ca, cb):
    return lax.dot_general(a, b, (((ca,), (cb,)), ((), ())), preferred_element_type=F32)


class Place:
    def __init__(self):
        c, d = lax.axis_index("ctx"), lax.axis_index("dp")
        self.zh, self.x, self.core = c // 8, (c % 8) // 2, c % 2
        self.zl, self.y = d // 4, d % 4

    def at(self, x=None, core=None, y=None, zl=None, zh=None):
        x = self.x if x is None else x
        core = self.core if core is None else core
        y = self.y if y is None else y
        zl = self.zl if zl is None else zl
        zh = self.zh if zh is None else zh
        return (zh * 8 + x * 2 + core, zl * 4 + y)


def both(*conds):
    total = conds[0]
    for cond in conds[1:]:
        total = jnp.logical_and(total, cond)
    return total


class Sends:
    def __init__(self, sems):
        self.sems, self.keys = sems, {}

    def start(self, key, cond, src, dst, recv_sem, device, whole):
        if key not in self.keys:
            self.keys[key] = (len(self.keys), cond, whole)
        copy = pltpu.make_async_remote_copy(
            src_ref=src, dst_ref=dst, send_sem=self.sems.at[self.keys[key][0]], recv_sem=recv_sem,
            device_id=device, device_id_type=MESH,
        )
        if cond is None:
            copy.start()
        else:
            pl.when(cond)(copy.start)

    def finish(self):
        for index, cond, whole in self.keys.values():
            def act(index=index, whole=whole):
                arrived(whole, self.sems.at[index])
            if cond is None:
                act()
            else:
                pl.when(cond)(act)


def arrived(dst, sem):
    pltpu.make_async_copy(dst, dst, sem).wait()


def local_copy(cond, src, dst, sem):
    copy = pltpu.make_async_copy(src, dst, sem)
    if cond is None:
        copy.start()
    else:
        pl.when(cond)(copy.start)


def signal(cond, sem, device):
    def act():
        pl.semaphore_signal(sem, inc=1, device_id=device, device_id_type=MESH)
    if cond is None:
        act()
    else:
        pl.when(cond)(act)


def number(cond):
    return jnp.where(cond, 1, 0).astype(jnp.int32)


def lanes_of(g, count=1):
    if isinstance(g, int):
        return pl.ds(g * HD, count * HD)
    return pl.ds(pl.multiple_of(g * HD, HD), count * HD)


def rows_of(j):
    return pl.ds(pl.multiple_of(j * QUARTER, QUARTER), QUARTER)


def ring(v, j):
    return (v + j) % 4


def fused_kernel(
    order_ref, q_hbm, do_hbm, k_hbm, v_hbm,
    attn_hbm, dq_hbm, dk_ref, dv_ref, of_ref, gf_ref,
    qv, dov, ov, dqv, kvs, dkv, gram, bias,
    rel, mate, snd, rel2, relsum, in1, in2,
    g0, ay, ry, ax, rx, az, rz, ah, rh,
    zown, order, cs, cr, ys, yr, xs, xr, zs, zr,
    ssem, qsem, outsem, ownsem, rsem, relsem, msem, rel2sem, in1sem, in2sem,
    o0sem, oysem, oxsem, ozsem, gsem, zsem, ready2, ready3,
):
    p = Place()
    x, core, y, zl, zh = p.x, p.core, p.y, p.zl, p.zh
    up, down, other = ring(zh, 1), ring(zh, 3), 1 - core
    own = (k_hbm, v_hbm)
    owner = jnp.logical_or(x == 3, both(x == 2, core == 1))
    blk = 2 * (x - 2) + core - 1
    bar = pltpu.get_barrier_semaphore()
    sends = Sends(ssem)

    core0, core1 = core == 0, core == 1
    x0, x_up, x0core0 = x == 0, x >= 1, both(x == 0, core == 0)
    on0, on1 = both(x <= 2, core == 0), both(x <= 2, core == 1)
    tail_at = {0: x0core0, 1: both(x == 1, core == 0)}
    two_up = both(core == 0, x >= 2)
    tall, thin, one_slot = mate.at[0], rel2.at[0], kvs.at[0, :, pl.ds(0, TOK), :]
    one_ay, one_ax, one_gc, one_gy, one_gx = ay.at[0], ax.at[0], cr, ys.at[0], xs.at[0]

    signal(None, bar, p.at(zh=up))
    signal(None, bar, p.at(zh=down))
    for j in range(4):
        signal(x == 0, bar, p.at(x=j, zh=down))
        signal(both(x == 0, core == 0), bar, p.at(x=j, core=1, zh=down))
        for t in range(2):
            signal(x == 3, bar, p.at(x=j, core=t, zh=up))
            signal(both(x == 2, core == 1), bar, p.at(x=j, core=t, zh=up))
    for j in (1, 2, 3):
        signal(None, bar, p.at(zl=ring(zl, j)))
        signal(None, bar, p.at(y=ring(y, j)))
    for j in range(4):
        for t in range(2):
            signal(jnp.logical_not(both(x == j, core == t)), bar, p.at(x=j, core=t))

    for g in range(KVH):
        heads = lanes_of(8 * g, 8)
        local_copy(None, q_hbm.at[:, heads], qv.at[:, heads], qsem.at[0, g])
        local_copy(None, do_hbm.at[:, heads], dov.at[:, heads], qsem.at[1, g])
        if g == 0:
            for kind in range(2):
                for i in range(KVH):
                    local_copy(None, own[kind].at[:, lanes_of(i)], kvs.at[kind, i, pl.ds(0, TOK), :], ownsem.at[kind])
    half = TOK // 2
    c = lax.axis_index("ctx")
    row = lax.broadcasted_iota(jnp.int32, (half, TOK), 0)
    col = lax.broadcasted_iota(jnp.int32, (half, TOK), 1)
    query_place = jnp.where(col < half, order_ref[2 * c] * half + col, order_ref[2 * c + 1] * half + (col - half))
    for s in range(STEPS):
        kc = (c - s + 32) % 32
        for part in range(2):
            key_place = order_ref[2 * kc + part] * half + row
            bias[pl.ds(s * TOK + part * half, half), :] = jnp.where(key_place <= query_place, 0.0, NEG).astype(F32)
    i = lax.broadcasted_iota(jnp.int32, (2 * HD, 2 * HD), 0)
    q = lax.broadcasted_iota(jnp.int32, (2 * HD, 2 * HD), 1)
    natural = ((q // 8) % 4) * 64 + (q // 128) * 32 + ((q // 2) % 4) * 8 + ((q // 32) % 4) * 2 + q % 2
    order[...] = jnp.where(i == natural, 1.0, 0.0).astype(BF)
    pl.semaphore_wait(bar, 7 + 3 + 3 + 2 + 1 + core + 3)

    def slot(kind, s, g):
        return kvs.at[kind, g, pl.ds(s * TOK, TOK), :]

    for kind in range(2):
        arrived(kvs.at[kind, :, pl.ds(0, TOK), :], ownsem.at[kind])

    for wide in range(2):
        group = pl.ds(0, 1) if wide == 0 else pl.ds(1, 3)
        for j in range(4):
            for t in range(2):
                mine = both(x == j, core == t)
                piece = kvs.at[t, group, pl.ds(j * QUARTER, QUARTER), :]
                target = rel.at[blk, group]
                sends.start(("spread", j, t), both(owner, jnp.logical_not(mine)), piece, target,
                            relsem.at[blk, wide], p.at(x=j, core=t), rel.at[0])
                local_copy(both(owner, mine), piece, target, relsem.at[blk, wide])
    for g in range(KVH):
        for kind in range(2):
            sends.start(("own", kind), core0, slot(kind, 0, g), slot(kind, 1, g), rsem.at[kind, 0, g],
                        p.at(core=1), one_slot)
    relay_in(rel, relsem, 0)
    relay_out(sends, p, rel, kvs, rsem, 0, up)
    relay_in(rel, relsem, 1)
    for g in range(1, KVH):
        relay_out(sends, p, rel, kvs, rsem, g, up)
    for g in range(KVH):
        for kind in range(2):
            s = 2 + kind - core
            sends.start(("near", kind), x <= 2, slot(kind, 0, g), slot(kind, s, g), rsem.at[kind, s - 1, g],
                        p.at(x=x + 1, core=kind), one_slot)
    for side in (up, down):
        signal(None, ready2, p.at(zh=side))

    def forward(g):
        for s in (1, 2):
            pl.when(core == 0)(lambda: arrived(slot(0, s, g), rsem.at[0, s - 1, g]))
            pl.when(core == 1)(lambda: arrived(slot(1, s + 1, g), rsem.at[1, s, g]))
            sends.start(("fk", s), core0, slot(0, s, g), slot(0, s + 1, g), rsem.at[0, s, g],
                        p.at(core=1), one_slot)
            sends.start(("fv", s), core1, slot(1, s + 1, g), slot(1, s, g), rsem.at[1, s - 1, g],
                        p.at(core=0), one_slot)
            if s == 1:
                sends.start(("f3k",), on0, slot(0, 1, g), slot(0, 3, g), rsem.at[0, 2, g],
                            p.at(x=x + 1, core=0), one_slot)
                sends.start(("f3v",), on1, slot(1, 2, g), slot(1, 3, g), rsem.at[1, 2, g],
                            p.at(x=x + 1, core=0), one_slot)

    def slots_ready(g):
        @pl.when(core == 0)
        def _():
            arrived(slot(0, 3, g), rsem.at[0, 2, g])
            for s in (1, 2, 3):
                arrived(slot(1, s, g), rsem.at[1, s - 1, g])

        @pl.when(core == 1)
        def _():
            arrived(slot(1, 1, g), rsem.at[1, 0, g])
            for s in (1, 2, 3):
                arrived(slot(0, s, g), rsem.at[0, s - 1, g])

    def compute(g):
        keys = kvs[0, g]
        values = kvs[1, g]
        q_all = jnp.concatenate([qv[:, lanes_of(8 * g + h)] for h in range(8)], axis=0)
        do_all = jnp.concatenate([dov[:, lanes_of(8 * g + h)] for h in range(8)], axis=0)
        mask = jnp.concatenate([bias[...], bias[...]], axis=1)
        probs, dscores = [], []
        for pair in range(4):
            cut = slice(pair * 2 * TOK, (pair + 1) * 2 * TOK)
            s = dot(keys, q_all[cut], 1, 1) * (SCALE * LOG2E) + mask
            dp = dot(values, do_all[cut], 1, 1)
            m = jnp.max(s, axis=0, keepdims=True)
            w = jnp.exp2(s - m)
            total = jnp.sum(w, axis=0, keepdims=True)
            mixed = jnp.sum(w * dp, axis=0, keepdims=True)
            inv = 1.0 / total
            delta = mixed * inv
            prob = w * inv
            probs.append(prob.astype(BF))
            dscores.append((prob * (dp - delta)).astype(BF))
        pb = jnp.concatenate(probs, axis=1)
        ds = jnp.concatenate(dscores, axis=1)
        dkv[1, g] = dot(pb, do_all, 1, 0).astype(BF)
        dkv[0, g] = (dot(ds, q_all, 1, 0) * SCALE).astype(BF)
        ot = dot(jnp.transpose(values), pb, 1, 0).astype(BF)
        dqt = (dot(jnp.transpose(keys), ds, 1, 0) * SCALE).astype(BF)
        for h in range(8):
            oh = ot[:, h * TOK:(h + 1) * TOK]
            ov[:, lanes_of(8 * g + h)] = jnp.transpose(oh)
            dqv[:, lanes_of(8 * g + h)] = jnp.transpose(dqt[:, h * TOK:(h + 1) * TOK])
            gram[h % 2, 4 * g + h // 2] = dot(oh, oh, 1, 1).astype(BF)
        heads = lanes_of(8 * g, 8)
        local_copy(None, ov.at[:, heads], attn_hbm.at[:, heads], outsem.at[0])
        local_copy(None, dqv.at[:, heads], dq_hbm.at[:, heads], outsem.at[1])

    def part(kind, s, g):
        return dkv.at[kind, g, pl.ds(s * TOK, TOK), :]

    def home1(g):
        for i in range(2):
            sends.start(("mv", i), core0, part(1, 1 + i, g), mate.at[i, g], msem.at[i, g], p.at(core=1), tall)
            sends.start(("mk", i), core1, part(0, 2 + i, g), mate.at[i, g], msem.at[i, g], p.at(core=0), tall)
        for kind in range(2):
            for j in range(4):
                piece = dkv.at[kind, g, pl.ds(3 * TOK + j * QUARTER, QUARTER), :]
                for sx, b in ((0, 2), (1, 3)):
                    here = tail_at[sx]
                    if kind == 0 and j == sx:
                        local_copy(here, piece, rel2.at[b, g], rel2sem.at[b, g])
                    else:
                        sends.start(("r3", kind, j, b), here, piece, rel2.at[b, g], rel2sem.at[b, g],
                                    p.at(x=j, core=kind), thin)
            sends.start(("m1", kind), core1, part(kind, 1, g), in2.at[kind, g], in2sem.at[kind, g], p.at(core=0), tall)
            sends.start(("m3", kind), two_up, part(kind, 3, g), in2.at[kind, g],
                        in2sem.at[kind, g], p.at(x=x - 2, core=1), tall)

    def home2(g):
        for i in range(2):
            arrived(mate.at[i, g], msem.at[i, g])
            rows = pl.ds(pl.multiple_of((1 + i + core) * TOK, TOK), TOK)
            mine = dkv[core, g, rows, :]
            snd[i, g] = (mine.astype(F32) + mate[i, g].astype(F32)).astype(BF)
            sends.start(("n", i), x_up, snd.at[i, g], in1.at[core, g], in1sem.at[core, g],
                        p.at(x=x - 1, core=1 - i), tall)
            for j in range(4):
                piece = snd.at[i, g, pl.ds(j * QUARTER, QUARTER), :]
                if j == 0:
                    local_copy(x0, piece, rel2.at[i, g], rel2sem.at[i, g])
                else:
                    sends.start(("r", i, j), x0, piece, rel2.at[i, g], rel2sem.at[i, g], p.at(x=j), thin)

    def home3(g):
        def there(ref):
            return ref.at[core, g, rows_of(x), :]

        arrived(rel2.at[2, g], rel2sem.at[2, g])
        sends.start(("h2",), None, rel2.at[2, g], there(in2), in2sem.at[core, g], p.at(x=2, core=1, zh=down), thin)
        arrived(rel2.at[1, g], rel2sem.at[1, g])
        sends.start(("h1",), None, rel2.at[1, g], there(in1), in1sem.at[core, g], p.at(x=3, core=0, zh=down), thin)
        arrived(rel2.at[0, g], rel2sem.at[0, g])
        arrived(rel2.at[3, g], rel2sem.at[3, g])
        relsum[g] = (
            rel2[0, g].astype(F32) + rel2[3, g].astype(F32)).astype(BF)
        sends.start(("h0",), None, relsum.at[g], there(in1), in1sem.at[core, g], p.at(x=3, core=1, zh=down), thin)

    last = both(x == 3, core == 1)
    outs = (dk_ref, dv_ref)

    def home4(g):
        for kind in range(2):
            arrived(in1.at[kind, g], in1sem.at[kind, g])
            near = dkv[kind, g, pl.ds(0, TOK), :].astype(F32) + in1[kind, g].astype(F32)

            @pl.when(last)
            def _():
                outs[kind][0, :, lanes_of(g)] = near.astype(BF)

            @pl.when(jnp.logical_not(last))
            def _():
                arrived(in2.at[kind, g], in2sem.at[kind, g])
                outs[kind][0, :, lanes_of(g)] = (near + in2[kind, g].astype(F32)).astype(BF)

            zown[g, :, pl.ds(kind * HD, HD)] = outs[kind][0, :, lanes_of(g)]

    def factor1(g):
        z = zown[g]
        ordered = dot(z, order[...], 1, 0).astype(BF)
        cs[g] = dot(ordered, z, 0, 0).reshape(2, 128, 2 * HD).astype(BF)
        sends.start(("gc",), None, cs.at[g, other], cr.at[g], gsem.at[g, 0], p.at(core=other), one_gc)

    def factor2(g):
        arrived(cr.at[g], gsem.at[g, 0])
        ys[g] = (cs[g, core].astype(F32) + cr[g].astype(F32)).reshape(4, 32, 2 * HD).astype(BF)
        for j in (1, 2, 3):
            sends.start(("gy", j), None, ys.at[g, ring(y, j)], yr.at[g, j - 1], gsem.at[g, j], p.at(y=ring(y, j)), one_gy)

    def factor3(g):
        total = ys[g, y].astype(F32)
        for j in range(3):
            arrived(yr.at[g, j], gsem.at[g, 1 + j])
            total = total + yr[g, j].astype(F32)
        xs[g] = total.reshape(4, 8, 2 * HD)
        for j in (1, 2, 3):
            sends.start(("gx", j), None, xs.at[g, ring(x, j)], xr.at[g, j - 1], gsem.at[g, 3 + j], p.at(x=ring(x, j)), one_gx)

    def factor4(g):
        total = xs[g, x]
        for j in range(3):
            arrived(xr.at[g, j], gsem.at[g, 4 + j])
            total = total + xr[g, j]
        mine = zh * 4 + zl
        for j in range(4):
            zs[g, j] = total[2 * j:2 * j + 2, :]
            here = both(zh == g, zl == j)
            sends.start(("gz", g, j), jnp.logical_not(here), zs.at[g, j], zr.at[mine], zsem.at[mine],
                        p.at(zh=g, zl=j), zs.at[g, j])
            local_copy(here, zs.at[g, j], zr.at[mine], zsem.at[mine])

    def out1(g):
        mine = pl.ds(4 * g, 4)
        sends.start(("oc",), None, gram.at[other, mine], g0.at[mine], o0sem.at[g], p.at(core=other), g0)

    def out2(g):
        arrived(g0.at[pl.ds(4 * g, 4)], o0sem.at[g])
        for h in range(4):
            pair_sum = gram[core, 4 * g + h].astype(F32) + g0[4 * g + h].astype(F32)
            split = pair_sum.reshape(4, 4, 8, HD)
            for j in range(4):
                ay[g, j, pl.ds(h * 32, 32), :] = split[:, j].reshape(32, HD).astype(BF)
        for j in (1, 2, 3):
            sends.start(("oy", j), None, ay.at[g, ring(y, j)], ry.at[g, j - 1], oysem.at[g, j - 1], p.at(y=ring(y, j)), one_ay)

    def out3(g):
        for j in range(3):
            arrived(ry.at[g, j], oysem.at[g, j])
        total = ay[g, y].astype(F32)
        for j in range(3):
            total = total + ry[g, j].astype(F32)
        ax[g] = total.reshape(4, 32, HD).astype(BF)
        for j in (1, 2, 3):
            sends.start(("ox", j), None, ax.at[g, ring(x, j)], rx.at[g, j - 1], oxsem.at[g, j - 1], p.at(x=ring(x, j)), one_ax)

    def out4(g):
        for j in range(3):
            arrived(rx.at[g, j], oxsem.at[g, j])
        total = ax[g, x].astype(F32)
        for j in range(3):
            total = total + rx[g, j].astype(F32)
        total = total.reshape(4, 8, HD)
        for j in range(4):
            az[j, g] = total[j]

    forward(0)

    def step(g, _):
        pl.when(g < 3)(lambda: forward(jnp.minimum(g + 1, 3)))
        slots_ready(g)
        heads = lanes_of(8 * g, 8)
        arrived(qv.at[:, heads], qsem.at[0, g])
        arrived(dov.at[:, heads], qsem.at[1, g])
        compute(g)
        home1(g)
        out1(g)

        @pl.when(g >= 1)
        def _():
            home2(g - 1)
            out2(g - 1)

        @pl.when(g >= 2)
        def _():
            home3(g - 2)
            out3(g - 2)

        @pl.when(g == 3)
        def _():
            home4(0)
            factor1(0)
            out4(0)
        return 0

    lax.fori_loop(0, KVH, step, 0)
    home2(3)
    home3(2)
    out2(3)
    out3(2)
    pl.semaphore_wait(ready2, 2)
    for j in (1, 2, 3):
        signal(None, ready3, p.at(zl=ring(zl, j)))
    home4(1)
    factor1(1)
    home3(3)
    factor2(0)
    out4(1)
    out3(3)
    home4(2)
    factor1(2)
    factor2(1)
    factor3(0)
    out4(2)
    out4(3)
    for j in (1, 2, 3):
        sends.start(("oz", j), None, az.at[ring(zl, j)], rz.at[j - 1], ozsem.at[j - 1], p.at(zl=ring(zl, j)), rz.at[0])
    home4(3)
    factor1(3)
    factor2(2)
    factor3(1)
    pl.semaphore_wait(ready3, 3)
    factor4(0)
    factor2(3)
    factor3(2)
    factor4(1)
    for j in range(3):
        arrived(rz.at[j], ozsem.at[j])
    ah[...] = az[zl] + rz[0] + rz[1] + rz[2]
    for j in (1, 2, 3):
        sends.start(("oh", j), None, ah.at[ring(zh, j)], rh.at[j - 1], ozsem.at[2 + j], p.at(zh=ring(zh, j)), rh.at[0])
    factor3(3)
    factor4(2)
    factor4(3)
    arrived(attn_hbm, outsem.at[0])
    arrived(dq_hbm, outsem.at[1])
    tokens = float(512 * TOK)
    for j in range(3):
        arrived(rh.at[j], ozsem.at[3 + j])
    of_ref[...] = (ah[zh] + rh[0] + rh[1] + rh[2]) / tokens
    sends.finish()
    total = jnp.zeros((2, 2 * HD), F32)
    for j in range(16):
        arrived(zr.at[j], zsem.at[j])
        total = total + zr[j]
    gf_ref[...] = total / tokens


def relay_in(rel, relsem, wide):
    group = pl.ds(0, 1) if wide == 0 else pl.ds(1, 3)
    for b in range(3):
        arrived(rel.at[b, group], relsem.at[b, wide])


def relay_out(sends, p, rel, kvs, rsem, g, up):
    for b in range(3):
        s = (3 - b) + (0 if b == 0 else p.core)
        rows = pl.ds(pl.multiple_of(s * TOK + p.x * QUARTER, QUARTER), QUARTER)
        sends.start(("relay", b), None, rel.at[b, g], kvs.at[p.core, g, rows, :],
                    rsem.at[p.core, s - 1, g], p.at(x=0, zh=up, core=0 if b == 0 else p.core), rel.at[0])


def fused(order, q, do, keys, values):
    vmem, hbm = pl.BlockSpec(memory_space=pltpu.VMEM), pl.BlockSpec(memory_space=pl.ANY)
    wide, all_lanes = KVH * HD, q.shape[1]
    V = pltpu.VMEM
    D = pltpu.SemaphoreType.DMA
    return pl.pallas_call(
        fused_kernel,
        out_shape=[
            jax.ShapeDtypeStruct((TOK, all_lanes), BF),
            jax.ShapeDtypeStruct((TOK, all_lanes), BF),
            jax.ShapeDtypeStruct((1, TOK, wide), BF),
            jax.ShapeDtypeStruct((1, TOK, wide), BF),
            jax.ShapeDtypeStruct((8, HD), F32),
            jax.ShapeDtypeStruct((2, 2 * HD), F32),
        ],
        in_specs=[pl.BlockSpec(memory_space=pltpu.SMEM)] + [hbm] * 4,
        out_specs=[hbm, hbm] + [vmem] * 4,
        scratch_shapes=[
            V((TOK, all_lanes), BF), V((TOK, all_lanes), BF), V((TOK, all_lanes), BF), V((TOK, all_lanes), BF),
            V((2, KVH, STEPS * TOK, HD), BF), V((2, KVH, STEPS * TOK, HD), BF),
            V((2, 16, HD, HD), BF), V((STEPS * TOK, TOK), F32),
            V((3, KVH, QUARTER, HD), BF), V((2, KVH, TOK, HD), BF), V((2, KVH, TOK, HD), BF),
            V((4, KVH, QUARTER, HD), BF), V((KVH, QUARTER, HD), BF), V((2, KVH, TOK, HD), BF), V((2, KVH, TOK, HD), BF),
            V((16, HD, HD), BF), V((4, 4, 128, HD), BF), V((4, 3, 128, HD), BF),
            V((4, 4, 32, HD), BF), V((4, 3, 32, HD), BF),
            V((4, 4, 8, HD), F32), V((3, 4, 8, HD), F32), V((4, 8, HD), F32), V((3, 8, HD), F32),
            V((4, TOK, 2 * HD), BF), V((2 * HD, 2 * HD), BF),
            V((4, 2, 128, 2 * HD), BF), V((4, 128, 2 * HD), BF),
            V((4, 4, 32, 2 * HD), BF), V((4, 3, 32, 2 * HD), BF),
            V((4, 4, 8, 2 * HD), F32), V((4, 3, 8, 2 * HD), F32),
            V((4, 4, 2, 2 * HD), F32), V((16, 2, 2 * HD), F32),
            D((96,)), D((2, 4)), D((2,)), D((2,)), D((2, 3, 4)), D((3, 2)), D((2, 4)), D((4, 4)), D((2, 4)), D((2, 4)),
            D((4,)), D((4, 3)), D((4, 3)), D((6,)), D((4, 7)), D((16,)),
            pltpu.SemaphoreType.REGULAR, pltpu.SemaphoreType.REGULAR,
        ],
        compiler_params=pltpu.CompilerParams(
            collective_id=0, has_side_effects=True, vmem_limit_bytes=60 * 2**20),
    )(order, q, do, keys, values)


def handover_kernel(*refs):
    count = len(refs) // 2
    for i in range(count):
        refs[count + i][...] = refs[i][...]


def handover(attn, dq, dk, dv, out_factor, grad_factor):
    arrays = (attn, dq, dk, dv, out_factor, grad_factor)
    steps = 4
    big = pl.BlockSpec((TOK, attn.shape[1] // steps), lambda i: (0, i))
    small = pl.BlockSpec((1, TOK, dk.shape[2] // steps), lambda i: (0, 0, i))
    whole = [pl.BlockSpec(a.shape, lambda i: (0, 0)) for a in (out_factor, grad_factor)]
    specs = [big, big, small, small] + whole
    return pl.pallas_call(
        handover_kernel,
        grid=(steps,),
        out_shape=[jax.ShapeDtypeStruct(a.shape, a.dtype) for a in arrays],
        in_specs=specs,
        out_specs=specs,
    )(*arrays)


def local(queries, key_heads, value_heads, out_grad, block_order):
    outs = fused(block_order, queries[0], out_grad[0], key_heads[0], value_heads[0])
    attn, dq, dk, dv, out_factor, grad_factor = handover(*outs)
    return attn[None], dq[None], dk, dv, out_factor, grad_factor


def solution(mesh):
    rows = P("dp", "ctx", None)
    return jax.shard_map(
        local,
        mesh=mesh,
        in_specs=(rows, rows, rows, rows, P()),
        out_specs=(rows, rows, rows, rows, P(("ctx", "dp"), None), P(("ctx", "dp"), None)),
        check_vma=False,
    )
```

```python
import math

import jax
import jax.numpy as jnp
from jax import lax
from jax.experimental import pallas as pl
from jax.experimental.pallas import tpu as pltpu
from jax.sharding import PartitionSpec as P

HD = 128
STEPS = 4
TOK = 128
QUARTER = TOK // 4
KVH = 4
NEG = -1e30
LOG2E = 1.0 / math.log(2.0)
SCALE = 1.0 / math.sqrt(HD)
MESH = pl.DeviceIdType.MESH
BF = jnp.bfloat16
F32 = jnp.float32


def dot(a, b, ca, cb):
    return lax.dot_general(a, b, (((ca,), (cb,)), ((), ())), preferred_element_type=F32)


class Place:
    def __init__(self):
        c, d = lax.axis_index("ctx"), lax.axis_index("dp")
        self.zh, self.x, self.core = c // 8, (c % 8) // 2, c % 2
        self.zl, self.y = d // 4, d % 4

    def at(self, x=None, core=None, y=None, zl=None, zh=None):
        x = self.x if x is None else x
        core = self.core if core is None else core
        y = self.y if y is None else y
        zl = self.zl if zl is None else zl
        zh = self.zh if zh is None else zh
        return (zh * 8 + x * 2 + core, zl * 4 + y)


def both(*conds):
    total = conds[0]
    for cond in conds[1:]:
        total = jnp.logical_and(total, cond)
    return total


class Sends:
    def __init__(self, sems):
        self.sems, self.keys, self.always = sems, {}, {}

    def start(self, key, cond, src, dst, recv_sem, device, whole):
        if key not in self.keys:
            self.keys[key] = (len(self.keys), self.always.get(key, cond), whole)
        copy = pltpu.make_async_remote_copy(
            src_ref=src, dst_ref=dst, send_sem=self.sems.at[self.keys[key][0]], recv_sem=recv_sem,
            device_id=device, device_id_type=MESH,
        )
        if cond is None:
            copy.start()
        else:
            pl.when(cond)(copy.start)

    def finish(self):
        for index, cond, whole in self.keys.values():
            def act(index=index, whole=whole):
                arrived(whole, self.sems.at[index])
            if cond is None:
                act()
            else:
                pl.when(cond)(act)


def arrived(dst, sem):
    pltpu.make_async_copy(dst, dst, sem).wait()


def local_copy(cond, src, dst, sem):
    copy = pltpu.make_async_copy(src, dst, sem)
    if cond is None:
        copy.start()
    else:
        pl.when(cond)(copy.start)


def signal(cond, sem, device):
    def act():
        pl.semaphore_signal(sem, inc=1, device_id=device, device_id_type=MESH)
    if cond is None:
        act()
    else:
        pl.when(cond)(act)


def number(cond):
    return jnp.where(cond, 1, 0).astype(jnp.int32)


def lanes_of(g, count=1):
    if isinstance(g, int):
        return pl.ds(g * HD, count * HD)
    return pl.ds(pl.multiple_of(g * HD, HD), count * HD)


def rows_of(j):
    return pl.ds(pl.multiple_of(j * QUARTER, QUARTER), QUARTER)


def ring(v, j):
    return (v + j) % 4


def fused_kernel(
    order_ref, q_hbm, do_hbm, k_hbm, v_hbm,
    attn_hbm, dq_hbm, dk_ref, dv_ref, of_ref, gf_ref,
    qv, dov, ov, dqv, kvs, dkv, gram, bias,
    rel, mate, snd, rel2, relsum, in1, in2,
    g0, ay, ry, ax, rx, az, rz, ah, rh,
    zown, order, cs, cr, ys, yr, xs, xr, zs, zr,
    ssem, qsem, outsem, ownsem, rsem, relsem, msem, rel2sem, in1sem, in2sem,
    o0sem, oysem, oxsem, ozsem, gsem, zsem, ready1, ready2, ready3,
):
    p = Place()
    x, core, y, zl, zh = p.x, p.core, p.y, p.zl, p.zh
    up, down, other = ring(zh, 1), ring(zh, 3), 1 - core
    own = (k_hbm, v_hbm)
    owner = jnp.logical_or(x == 3, both(x == 2, core == 1))
    blk = 2 * (x - 2) + core - 1
    bar = pltpu.get_barrier_semaphore()
    sends = Sends(ssem)
    sends.always = {"spread": owner, "gz": None}

    core0, core1 = core == 0, core == 1
    x0, x_up, x0core0 = x == 0, x >= 1, both(x == 0, core == 0)
    on0, on1 = both(x <= 2, core == 0), both(x <= 2, core == 1)
    tail_at = {0: x0core0, 1: both(x == 1, core == 0)}
    two_up = both(core == 0, x >= 2)
    blocks = {n: gram.at[0, pl.ds(0, n)] for n in (3, 4, 6, 7, 8, 12, 16)}
    blocks[24] = kvs.at[:, pl.ds(0, 3)]
    all_z = zr.at[pl.ds(0, 15)]

    signal(None, bar, p.at(zh=up))
    signal(None, bar, p.at(zh=down))
    for j in (1, 2, 3):
        signal(None, bar, p.at(zl=ring(zl, j)))
        signal(None, bar, p.at(y=ring(y, j)))
    for j in range(4):
        for t in range(2):
            signal(jnp.logical_not(both(x == j, core == t)), bar, p.at(x=j, core=t))

    for g in range(KVH):
        heads = lanes_of(8 * g, 8)
        local_copy(None, q_hbm.at[:, heads], qv.at[:, heads], qsem.at[0, g])
        local_copy(None, do_hbm.at[:, heads], dov.at[:, heads], qsem.at[1, g])
        if g == 0:
            for kind in range(2):
                for i in range(KVH):
                    local_copy(None, own[kind].at[:, lanes_of(i)], kvs.at[kind, i, pl.ds(0, TOK), :], ownsem.at[kind])
    half = TOK // 2
    c = lax.axis_index("ctx")
    row = lax.broadcasted_iota(jnp.int32, (half, TOK), 0)
    col = lax.broadcasted_iota(jnp.int32, (half, TOK), 1)
    query_place = jnp.where(col < half, order_ref[2 * c] * half + col, order_ref[2 * c + 1] * half + (col - half))
    for s in range(STEPS):
        kc = (c - s + 32) % 32
        for part in range(2):
            key_place = order_ref[2 * kc + part] * half + row
            bias[pl.ds(s * TOK + part * half, half), :] = jnp.where(key_place <= query_place, 0.0, NEG).astype(F32)
    i = lax.broadcasted_iota(jnp.int32, (2 * HD, 2 * HD), 0)
    q = lax.broadcasted_iota(jnp.int32, (2 * HD, 2 * HD), 1)
    natural = ((q // 8) % 4) * 64 + (q // 128) * 32 + ((q // 2) % 4) * 8 + ((q // 32) % 4) * 2 + q % 2
    order[...] = jnp.where(i == natural, 1.0, 0.0).astype(BF)
    pl.semaphore_wait(bar, 7 + 3 + 3 + 2)

    def slot(kind, s, g):
        return kvs.at[kind, g, pl.ds(s * TOK, TOK), :]

    for kind in range(2):
        arrived(kvs.at[kind, :, pl.ds(0, TOK), :], ownsem.at[kind])

    for wide in range(2):
        group = pl.ds(0, 1) if wide == 0 else pl.ds(1, 3)
        for j in range(4):
            for t in range(2):
                mine = both(x == j, core == t)
                piece = kvs.at[t, group, pl.ds(j * QUARTER, QUARTER), :]
                target = rel.at[blk, group]
                sends.start("spread", both(owner, jnp.logical_not(mine)), piece, target,
                            relsem.at[blk, wide], p.at(x=j, core=t), blocks[7])
                local_copy(both(owner, mine), piece, target, relsem.at[blk, wide])
    for j in range(4):
        for t in range(2):
            signal(jnp.logical_not(both(x == j, core == t)), ready1, p.at(x=j, core=t))
    for g in range(KVH):
        for kind in range(2):
            sends.start("core0", core0, slot(kind, 0, g), slot(kind, 1, g), rsem.at[kind, 0, g],
                        p.at(core=1), blocks[24])
    for g in range(2):
        for kind in range(2):
            s = 2 + kind - core
            sends.start("near", x <= 2, slot(kind, 0, g), slot(kind, s, g), rsem.at[kind, s - 1, g],
                        p.at(x=x + 1, core=kind), blocks[8])
    pl.semaphore_wait(ready1, 7)
    relay_in(rel, relsem, 0)
    relay_out(sends, p, rel, kvs, rsem, 0, up, blocks[3])
    relay_in(rel, relsem, 1)
    for g in range(1, KVH):
        relay_out(sends, p, rel, kvs, rsem, g, up, blocks[3])
    for g in range(2, KVH):
        for kind in range(2):
            s = 2 + kind - core
            sends.start("near", x <= 2, slot(kind, 0, g), slot(kind, s, g), rsem.at[kind, s - 1, g],
                        p.at(x=x + 1, core=kind), blocks[8])
    for side in (up, down):
        signal(None, ready2, p.at(zh=side))

    def forward(g):
        for s in (1, 2):
            pl.when(core == 0)(lambda: arrived(slot(0, s, g), rsem.at[0, s - 1, g]))
            pl.when(core == 1)(lambda: arrived(slot(1, s + 1, g), rsem.at[1, s, g]))
            sends.start("core0", core0, slot(0, s, g), slot(0, s + 1, g), rsem.at[0, s, g],
                        p.at(core=1), blocks[24])
            sends.start("core1", core1, slot(1, s + 1, g), slot(1, s, g), rsem.at[1, s - 1, g],
                        p.at(core=0), blocks[24])
            if s == 1:
                sends.start("f3k", on0, slot(0, 1, g), slot(0, 3, g), rsem.at[0, 2, g],
                            p.at(x=x + 1, core=0), blocks[4])
                sends.start("f3v", on1, slot(1, 2, g), slot(1, 3, g), rsem.at[1, 2, g],
                            p.at(x=x + 1, core=0), blocks[4])

    def slots_ready(g):
        @pl.when(core == 0)
        def _():
            arrived(slot(0, 3, g), rsem.at[0, 2, g])
            for s in (1, 2, 3):
                arrived(slot(1, s, g), rsem.at[1, s - 1, g])

        @pl.when(core == 1)
        def _():
            arrived(slot(1, 1, g), rsem.at[1, 0, g])
            for s in (1, 2, 3):
                arrived(slot(0, s, g), rsem.at[0, s - 1, g])

    def compute(g):
        keys = kvs[0, g]
        values = kvs[1, g]
        q_all = jnp.concatenate([qv[:, lanes_of(8 * g + h)] for h in range(8)], axis=0)
        do_all = jnp.concatenate([dov[:, lanes_of(8 * g + h)] for h in range(8)], axis=0)
        mask = jnp.concatenate([bias[...], bias[...]], axis=1)
        probs, dscores = [], []
        for pair in range(4):
            cut = slice(pair * 2 * TOK, (pair + 1) * 2 * TOK)
            s = dot(keys, q_all[cut], 1, 1) * (SCALE * LOG2E) + mask
            dp = dot(values, do_all[cut], 1, 1)
            m = jnp.max(s, axis=0, keepdims=True)
            w = jnp.exp2(s - m)
            total = jnp.sum(w, axis=0, keepdims=True)
            mixed = jnp.sum(w * dp, axis=0, keepdims=True)
            inv = 1.0 / total
            delta = mixed * inv
            prob = w * inv
            probs.append(prob.astype(BF))
            dscores.append((prob * (dp - delta)).astype(BF))
        pb = jnp.concatenate(probs, axis=1)
        ds = jnp.concatenate(dscores, axis=1)
        dkv[1, g] = dot(pb, do_all, 1, 0).astype(BF)
        dkv[0, g] = (dot(ds, q_all, 1, 0) * SCALE).astype(BF)
        home1(g)
        ot = dot(jnp.transpose(values), pb, 1, 0).astype(BF)
        dqt = (dot(jnp.transpose(keys), ds, 1, 0) * SCALE).astype(BF)
        for h in range(8):
            oh = ot[:, h * TOK:(h + 1) * TOK]
            ov[:, lanes_of(8 * g + h)] = jnp.transpose(oh)
            dqv[:, lanes_of(8 * g + h)] = jnp.transpose(dqt[:, h * TOK:(h + 1) * TOK])
            gram[h % 2, 4 * g + h // 2] = dot(oh, oh, 1, 1).astype(BF)
        heads = lanes_of(8 * g, 8)
        local_copy(None, ov.at[:, heads], attn_hbm.at[:, heads], outsem.at[0])
        local_copy(None, dqv.at[:, heads], dq_hbm.at[:, heads], outsem.at[1])

    def part(kind, s, g):
        return dkv.at[kind, g, pl.ds(s * TOK, TOK), :]

    def home1(g):
        for i in range(2):
            sends.start("core0", core0, part(1, 1 + i, g), mate.at[i, g], msem.at[i, g], p.at(core=1), blocks[24])
            sends.start("core1", core1, part(0, 2 + i, g), mate.at[i, g], msem.at[i, g], p.at(core=0), blocks[24])
        for kind in range(2):
            for j in range(4):
                piece = dkv.at[kind, g, pl.ds(3 * TOK + j * QUARTER, QUARTER), :]
                for sx, b in ((0, 2), (1, 3)):
                    here = tail_at[sx]
                    if kind == 0 and j == sx:
                        local_copy(here, piece, rel2.at[b, g], rel2sem.at[b, g])
                    else:
                        sends.start(("tail", sx), here, piece, rel2.at[b, g], rel2sem.at[b, g],
                                    p.at(x=j, core=kind), blocks[7])
            sends.start("core1", core1, part(kind, 1, g), in2.at[kind, g], in2sem.at[kind, g], p.at(core=0), blocks[24])
            sends.start("m3", two_up, part(kind, 3, g), in2.at[kind, g],
                        in2sem.at[kind, g], p.at(x=x - 2, core=1), blocks[8])

    def home2(g):
        for i in range(2):
            arrived(mate.at[i, g], msem.at[i, g])
            rows = pl.ds(pl.multiple_of((1 + i + core) * TOK, TOK), TOK)
            mine = dkv[core, g, rows, :]
            snd[i, g] = (mine.astype(F32) + mate[i, g].astype(F32)).astype(BF)
            sends.start("n", x_up, snd.at[i, g], in1.at[core, g], in1sem.at[core, g],
                        p.at(x=x - 1, core=1 - i), blocks[8])
            for j in range(4):
                piece = snd.at[i, g, pl.ds(j * QUARTER, QUARTER), :]
                if j == 0:
                    local_copy(x0, piece, rel2.at[i, g], rel2sem.at[i, g])
                else:
                    sends.start("r", x0, piece, rel2.at[i, g], rel2sem.at[i, g], p.at(x=j), blocks[6])

    def home3(g):
        def there(ref):
            return ref.at[core, g, rows_of(x), :]

        arrived(rel2.at[2, g], rel2sem.at[2, g])
        sends.start("home", None, rel2.at[2, g], there(in2), in2sem.at[core, g], p.at(x=2, core=1, zh=down), blocks[3])
        arrived(rel2.at[1, g], rel2sem.at[1, g])
        sends.start("home", None, rel2.at[1, g], there(in1), in1sem.at[core, g], p.at(x=3, core=0, zh=down), blocks[3])
        arrived(rel2.at[0, g], rel2sem.at[0, g])
        arrived(rel2.at[3, g], rel2sem.at[3, g])
        relsum[g] = (
            rel2[0, g].astype(F32) + rel2[3, g].astype(F32)).astype(BF)
        sends.start("home", None, relsum.at[g], there(in1), in1sem.at[core, g], p.at(x=3, core=1, zh=down), blocks[3])

    last = both(x == 3, core == 1)
    outs = (dk_ref, dv_ref)

    def home4(g):
        for kind in range(2):
            arrived(in1.at[kind, g], in1sem.at[kind, g])
            near = dkv[kind, g, pl.ds(0, TOK), :].astype(F32) + in1[kind, g].astype(F32)

            @pl.when(last)
            def _():
                outs[kind][0, :, lanes_of(g)] = near.astype(BF)

            @pl.when(jnp.logical_not(last))
            def _():
                arrived(in2.at[kind, g], in2sem.at[kind, g])
                outs[kind][0, :, lanes_of(g)] = (near + in2[kind, g].astype(F32)).astype(BF)

            zown[g, :, pl.ds(kind * HD, HD)] = outs[kind][0, :, lanes_of(g)]

    def factor1(g):
        z = zown[g]
        ordered = dot(z, order[...], 1, 0).astype(BF)
        cs[g] = dot(ordered, z, 0, 0).reshape(2, 128, 2 * HD).astype(BF)
        sends.start("gc", None, cs.at[g, other], cr.at[g], gsem.at[g, 0], p.at(core=other), blocks[8])

    def factor2(g):
        arrived(cr.at[g], gsem.at[g, 0])
        ys[g] = (cs[g, core].astype(F32) + cr[g].astype(F32)).reshape(4, 32, 2 * HD).astype(BF)
        for j in (1, 2, 3):
            sends.start("gy", None, ys.at[g, ring(y, j)], yr.at[g, j - 1], gsem.at[g, 1], p.at(y=ring(y, j)), blocks[6])

    def factor3(g):
        arrived(yr.at[g], gsem.at[g, 1])
        total = ys[g, y].astype(F32)
        for j in range(3):
            total = total + yr[g, j].astype(F32)
        xs[g] = total.reshape(4, 8, 2 * HD)
        for j in (1, 2, 3):
            sends.start("gx", None, xs.at[g, ring(x, j)], xr.at[g, j - 1], gsem.at[g, 2], p.at(x=ring(x, j)), blocks[3])

    def factor4(g):
        arrived(xr.at[g], gsem.at[g, 2])
        total = xs[g, x]
        for j in range(3):
            total = total + xr[g, j]
        mine = zh * 4 + zl
        for j in range(4):
            zs[g, j] = total[2 * j:2 * j + 2, :]
            here = both(zh == g, zl == j)
            sends.start("gz", jnp.logical_not(here), zs.at[g, j], zr.at[mine], zsem.at[0],
                        p.at(zh=g, zl=j), all_z)
            local_copy(here, zs.at[g, j], zr.at[mine], zsem.at[0])

    def out1(g):
        mine = pl.ds(4 * g, 4)
        sends.start("oc", None, gram.at[other, mine], g0.at[mine], o0sem.at[g], p.at(core=other), blocks[16])

    def out2(g):
        arrived(g0.at[pl.ds(4 * g, 4)], o0sem.at[g])
        for h in range(4):
            pair_sum = gram[core, 4 * g + h].astype(F32) + g0[4 * g + h].astype(F32)
            split = pair_sum.reshape(4, 4, 8, HD)
            for j in range(4):
                ay[g, j, pl.ds(h * 32, 32), :] = split[:, j].reshape(32, HD).astype(BF)
        for j in (1, 2, 3):
            sends.start("oy", None, ay.at[g, ring(y, j)], ry.at[g, j - 1], oysem.at[g], p.at(y=ring(y, j)), blocks[12])

    def out3(g):
        arrived(ry.at[g], oysem.at[g])
        total = ay[g, y].astype(F32)
        for j in range(3):
            total = total + ry[g, j].astype(F32)
        ax[g] = total.reshape(4, 32, HD).astype(BF)
        for j in (1, 2, 3):
            sends.start("ox", None, ax.at[g, ring(x, j)], rx.at[g, j - 1], oxsem.at[g], p.at(x=ring(x, j)), blocks[3])

    def out4(g):
        arrived(rx.at[g], oxsem.at[g])
        total = ax[g, x].astype(F32)
        for j in range(3):
            total = total + rx[g, j].astype(F32)
        total = total.reshape(4, 8, HD)
        for j in range(4):
            az[j, g] = total[j]

    forward(0)

    def step(g, _):
        pl.when(g < 3)(lambda: forward(jnp.minimum(g + 1, 3)))
        slots_ready(g)
        heads = lanes_of(8 * g, 8)
        arrived(qv.at[:, heads], qsem.at[0, g])
        arrived(dov.at[:, heads], qsem.at[1, g])
        compute(g)
        out1(g)

        @pl.when(g >= 1)
        def _():
            home2(g - 1)
            out2(g - 1)

        @pl.when(g >= 2)
        def _():
            home3(g - 2)
            out3(g - 2)

        @pl.when(g == 3)
        def _():
            home4(0)
            factor1(0)
            out4(0)
        return 0

    lax.fori_loop(0, KVH, step, 0)
    home2(3)
    home3(2)
    out2(3)
    out3(2)
    pl.semaphore_wait(ready2, 2)
    for j in (1, 2, 3):
        signal(None, ready3, p.at(zl=ring(zl, j)))
    home4(1)
    factor1(1)
    home3(3)
    factor2(0)
    out4(1)
    out3(3)
    home4(2)
    factor1(2)
    factor2(1)
    factor3(0)
    out4(2)
    out4(3)
    for j in (1, 2, 3):
        sends.start("oz", None, az.at[ring(zl, j)], rz.at[j - 1], ozsem.at[0], p.at(zl=ring(zl, j)), rz)
    home4(3)
    factor1(3)
    factor2(2)
    factor3(1)
    pl.semaphore_wait(ready3, 3)
    factor4(0)
    factor2(3)
    factor3(2)
    factor4(1)
    arrived(rz, ozsem.at[0])
    ah[...] = az[zl] + rz[0] + rz[1] + rz[2]
    for j in (1, 2, 3):
        sends.start("oh", None, ah.at[ring(zh, j)], rh.at[j - 1], ozsem.at[1], p.at(zh=ring(zh, j)), rh)
    factor3(3)
    factor4(2)
    factor4(3)
    arrived(attn_hbm, outsem.at[0])
    arrived(dq_hbm, outsem.at[1])
    tokens = float(512 * TOK)
    arrived(rh, ozsem.at[1])
    of_ref[...] = (ah[zh] + rh[0] + rh[1] + rh[2]) / tokens
    sends.finish()
    total = jnp.zeros((2, 2 * HD), F32)
    arrived(zr, zsem.at[0])
    for j in range(16):
        total = total + zr[j]
    gf_ref[...] = total / tokens


def relay_in(rel, relsem, wide):
    group = pl.ds(0, 1) if wide == 0 else pl.ds(1, 3)
    for b in range(3):
        arrived(rel.at[b, group], relsem.at[b, wide])


def relay_out(sends, p, rel, kvs, rsem, g, up, relayed):
    for b in range(3):
        s = (3 - b) + (0 if b == 0 else p.core)
        rows = pl.ds(pl.multiple_of(s * TOK + p.x * QUARTER, QUARTER), QUARTER)
        sends.start("relay", None, rel.at[b, g], kvs.at[p.core, g, rows, :],
                    rsem.at[p.core, s - 1, g], p.at(x=0, zh=up, core=0 if b == 0 else p.core), relayed)


def fused(order, q, do, keys, values):
    vmem, hbm = pl.BlockSpec(memory_space=pltpu.VMEM), pl.BlockSpec(memory_space=pl.ANY)
    wide, all_lanes = KVH * HD, q.shape[1]
    V = pltpu.VMEM
    D = pltpu.SemaphoreType.DMA
    return pl.pallas_call(
        fused_kernel,
        out_shape=[
            jax.ShapeDtypeStruct((TOK, all_lanes), BF),
            jax.ShapeDtypeStruct((TOK, all_lanes), BF),
            jax.ShapeDtypeStruct((1, TOK, wide), BF),
            jax.ShapeDtypeStruct((1, TOK, wide), BF),
            jax.ShapeDtypeStruct((8, HD), F32),
            jax.ShapeDtypeStruct((2, 2 * HD), F32),
        ],
        in_specs=[pl.BlockSpec(memory_space=pltpu.SMEM)] + [hbm] * 4,
        out_specs=[hbm, hbm] + [vmem] * 4,
        scratch_shapes=[
            V((TOK, all_lanes), BF), V((TOK, all_lanes), BF), V((TOK, all_lanes), BF), V((TOK, all_lanes), BF),
            V((2, KVH, STEPS * TOK, HD), BF), V((2, KVH, STEPS * TOK, HD), BF),
            V((2, 16, HD, HD), BF), V((STEPS * TOK, TOK), F32),
            V((3, KVH, QUARTER, HD), BF), V((2, KVH, TOK, HD), BF), V((2, KVH, TOK, HD), BF),
            V((4, KVH, QUARTER, HD), BF), V((KVH, QUARTER, HD), BF), V((2, KVH, TOK, HD), BF), V((2, KVH, TOK, HD), BF),
            V((16, HD, HD), BF), V((4, 4, 128, HD), BF), V((4, 3, 128, HD), BF),
            V((4, 4, 32, HD), BF), V((4, 3, 32, HD), BF),
            V((4, 4, 8, HD), F32), V((3, 4, 8, HD), F32), V((4, 8, HD), F32), V((3, 8, HD), F32),
            V((4, TOK, 2 * HD), BF), V((2 * HD, 2 * HD), BF),
            V((4, 2, 128, 2 * HD), BF), V((4, 128, 2 * HD), BF),
            V((4, 4, 32, 2 * HD), BF), V((4, 3, 32, 2 * HD), BF),
            V((4, 4, 8, 2 * HD), F32), V((4, 3, 8, 2 * HD), F32),
            V((4, 4, 2, 2 * HD), F32), V((16, 2, 2 * HD), F32),
            D((24,)), D((2, 4)), D((2,)), D((2,)), D((2, 3, 4)), D((3, 2)), D((2, 4)), D((4, 4)), D((2, 4)), D((2, 4)),
            D((4,)), D((4,)), D((4,)), D((2,)), D((4, 3)), D((1,)),
            pltpu.SemaphoreType.REGULAR, pltpu.SemaphoreType.REGULAR, pltpu.SemaphoreType.REGULAR,
        ],
        compiler_params=pltpu.CompilerParams(
            collective_id=0, has_side_effects=True, vmem_limit_bytes=60 * 2**20),
    )(order, q, do, keys, values)


def handover_kernel(*refs):
    count = len(refs) // 2
    for i in range(count):
        refs[count + i][...] = refs[i][...]


def handover(attn, dq, dk, dv, out_factor, grad_factor):
    arrays = (attn, dq, dk, dv, out_factor, grad_factor)
    steps = 2
    big = pl.BlockSpec((TOK // steps, attn.shape[1]), lambda i: (i, 0))
    small = pl.BlockSpec((1, TOK // steps, dk.shape[2]), lambda i: (0, i, 0))
    whole = [pl.BlockSpec(a.shape, lambda i: (0, 0)) for a in (out_factor, grad_factor)]
    specs = [big, big, small, small] + whole
    return pl.pallas_call(
        handover_kernel,
        grid=(steps,),
        out_shape=[jax.ShapeDtypeStruct(a.shape, a.dtype) for a in arrays],
        in_specs=specs,
        out_specs=specs,
    )(*arrays)


def local(queries, key_heads, value_heads, out_grad, block_order):
    outs = fused(block_order, queries[0], out_grad[0], key_heads[0], value_heads[0])
    attn, dq, dk, dv, out_factor, grad_factor = handover(*outs)
    return attn[None], dq[None], dk, dv, out_factor, grad_factor


def solution(mesh):
    rows = P("dp", "ctx", None)
    return jax.shard_map(
        local,
        mesh=mesh,
        in_specs=(rows, rows, rows, rows, P()),
        out_specs=(rows, rows, rows, rows, P(("ctx", "dp"), None), P(("ctx", "dp"), None)),
        check_vma=False,
    )
```

```python
import math

import jax
import jax.numpy as jnp
from jax import lax
from jax.experimental import pallas as pl
from jax.experimental.pallas import tpu as pltpu
from jax.sharding import PartitionSpec as P

HD = 128
STEPS = 4
TOK = 128
QUARTER = TOK // 4
KVH = 4
NEG = -1e30
LOG2E = 1.0 / math.log(2.0)
SCALE = 1.0 / math.sqrt(HD)
MESH = pl.DeviceIdType.MESH
BF = jnp.bfloat16
F32 = jnp.float32


def dot(a, b, ca, cb):
    return lax.dot_general(a, b, (((ca,), (cb,)), ((), ())), preferred_element_type=F32)


class Place:
    def __init__(self):
        c, d = lax.axis_index("ctx"), lax.axis_index("dp")
        self.zh, self.x, self.core = c // 8, (c % 8) // 2, c % 2
        self.zl, self.y = d // 4, d % 4

    def at(self, x=None, core=None, y=None, zl=None, zh=None):
        x = self.x if x is None else x
        core = self.core if core is None else core
        y = self.y if y is None else y
        zl = self.zl if zl is None else zl
        zh = self.zh if zh is None else zh
        return (zh * 8 + x * 2 + core, zl * 4 + y)


def both(*conds):
    total = conds[0]
    for cond in conds[1:]:
        total = jnp.logical_and(total, cond)
    return total


class Sends:
    def __init__(self, sems):
        self.sems, self.keys, self.always = sems, {}, {}

    def start(self, key, cond, src, dst, recv_sem, device, whole):
        if key not in self.keys:
            self.keys[key] = (len(self.keys), self.always.get(key, cond), whole)
        copy = pltpu.make_async_remote_copy(
            src_ref=src, dst_ref=dst, send_sem=self.sems.at[self.keys[key][0]], recv_sem=recv_sem,
            device_id=device, device_id_type=MESH,
        )
        if cond is None:
            copy.start()
        else:
            pl.when(cond)(copy.start)

    def finish(self):
        for index, cond, whole in self.keys.values():
            def act(index=index, whole=whole):
                arrived(whole, self.sems.at[index])
            if cond is None:
                act()
            else:
                pl.when(cond)(act)


def arrived(dst, sem):
    pltpu.make_async_copy(dst, dst, sem).wait()


def local_copy(cond, src, dst, sem):
    copy = pltpu.make_async_copy(src, dst, sem)
    if cond is None:
        copy.start()
    else:
        pl.when(cond)(copy.start)


def signal(cond, sem, device):
    def act():
        pl.semaphore_signal(sem, inc=1, device_id=device, device_id_type=MESH)
    if cond is None:
        act()
    else:
        pl.when(cond)(act)


def number(cond):
    return jnp.where(cond, 1, 0).astype(jnp.int32)


def lanes_of(g, count=1):
    if isinstance(g, int):
        return pl.ds(g * HD, count * HD)
    return pl.ds(pl.multiple_of(g * HD, HD), count * HD)


def rows_of(j):
    return pl.ds(pl.multiple_of(j * QUARTER, QUARTER), QUARTER)


def ring(v, j):
    return (v + j) % 4


def fused_kernel(
    order_hbm, q_hbm, do_hbm, k_hbm, v_hbm,
    attn_hbm, dq_hbm, dk_ref, dv_ref, of_ref, gf_ref,
    order_ref, qv, dov, ov, dqv, kvs, dkv, gram, bias,
    rel, mate, snd, rel2, relsum, in1, in2,
    g0, ay, ry, ax, rx, az, rz, ah, rh,
    zown, order, cs, cr, ys, yr, xs, xr, zs, zr,
    ssem, qsem, ordersem, outsem, ownsem, rsem, relsem, msem, rel2sem, in1sem, in2sem,
    o0sem, oysem, oxsem, ozsem, gsem, zsem, ready1, ready2, ready3,
):
    p = Place()
    x, core, y, zl, zh = p.x, p.core, p.y, p.zl, p.zh
    up, down, other = ring(zh, 1), ring(zh, 3), 1 - core
    own = (k_hbm, v_hbm)
    owner = jnp.logical_or(x == 3, both(x == 2, core == 1))
    blk = 2 * (x - 2) + core - 1
    bar = pltpu.get_barrier_semaphore()
    sends = Sends(ssem)
    sends.always = {"spread": owner, "gz": None}

    core0, core1 = core == 0, core == 1
    x0, x_up, x0core0 = x == 0, x >= 1, both(x == 0, core == 0)
    on0, on1 = both(x <= 2, core == 0), both(x <= 2, core == 1)
    tail_at = {0: x0core0, 1: both(x == 1, core == 0)}
    two_up = both(core == 0, x >= 2)
    blocks = {n: gram.at[0, pl.ds(0, n)] for n in (3, 4, 6, 7, 8, 12, 16)}
    blocks[24] = kvs.at[:, pl.ds(0, 3)]
    all_z = zr.at[pl.ds(0, 15)]

    local_copy(None, order_hbm, order_ref, ordersem.at[0])
    signal(None, bar, p.at(zh=up))
    signal(None, bar, p.at(zh=down))
    for j in (1, 2, 3):
        signal(None, bar, p.at(zl=ring(zl, j)))
        signal(None, bar, p.at(y=ring(y, j)))
    for j in range(4):
        for t in range(2):
            signal(jnp.logical_not(both(x == j, core == t)), bar, p.at(x=j, core=t))

    for g in range(KVH):
        heads = lanes_of(8 * g, 8)
        local_copy(None, q_hbm.at[:, heads], qv.at[:, heads], qsem.at[0, g])
        local_copy(None, do_hbm.at[:, heads], dov.at[:, heads], qsem.at[1, g])
        if g == 0:
            for kind in range(2):
                for i in range(KVH):
                    local_copy(None, own[kind].at[:, lanes_of(i)], kvs.at[kind, i, pl.ds(0, TOK), :], ownsem.at[kind])
    arrived(order_ref, ordersem.at[0])
    half = TOK // 2
    c = lax.axis_index("ctx")
    row = lax.broadcasted_iota(jnp.int32, (half, TOK), 0)
    col = lax.broadcasted_iota(jnp.int32, (half, TOK), 1)
    query_place = jnp.where(col < half, order_ref[2 * c] * half + col, order_ref[2 * c + 1] * half + (col - half))
    for s in range(STEPS):
        kc = (c - s + 32) % 32
        for part in range(2):
            key_place = order_ref[2 * kc + part] * half + row
            bias[pl.ds(s * TOK + part * half, half), :] = jnp.where(key_place <= query_place, 0.0, NEG).astype(F32)
    i = lax.broadcasted_iota(jnp.int32, (2 * HD, 2 * HD), 0)
    q = lax.broadcasted_iota(jnp.int32, (2 * HD, 2 * HD), 1)
    natural = ((q // 8) % 4) * 64 + (q // 128) * 32 + ((q // 2) % 4) * 8 + ((q // 32) % 4) * 2 + q % 2
    order[...] = jnp.where(i == natural, 1.0, 0.0).astype(BF)
    pl.semaphore_wait(bar, 7 + 3 + 3 + 2)

    def slot(kind, s, g):
        return kvs.at[kind, g, pl.ds(s * TOK, TOK), :]

    for kind in range(2):
        arrived(kvs.at[kind, :, pl.ds(0, TOK), :], ownsem.at[kind])

    for wide in range(2):
        group = pl.ds(0, 1) if wide == 0 else pl.ds(1, 3)
        for j in range(4):
            for t in range(2):
                mine = both(x == j, core == t)
                piece = kvs.at[t, group, pl.ds(j * QUARTER, QUARTER), :]
                target = rel.at[blk, group]
                sends.start("spread", both(owner, jnp.logical_not(mine)), piece, target,
                            relsem.at[blk, wide], p.at(x=j, core=t), blocks[7])
                local_copy(both(owner, mine), piece, target, relsem.at[blk, wide])
    for j in range(4):
        for t in range(2):
            signal(jnp.logical_not(both(x == j, core == t)), ready1, p.at(x=j, core=t))
    for g in range(KVH):
        for kind in range(2):
            sends.start("core0", core0, slot(kind, 0, g), slot(kind, 1, g), rsem.at[kind, 0, g],
                        p.at(core=1), blocks[24])
    for g in range(2):
        for kind in range(2):
            s = 2 + kind - core
            sends.start("near", x <= 2, slot(kind, 0, g), slot(kind, s, g), rsem.at[kind, s - 1, g],
                        p.at(x=x + 1, core=kind), blocks[8])
    pl.semaphore_wait(ready1, 7)
    relay_in(rel, relsem, 0)
    relay_out(sends, p, rel, kvs, rsem, 0, up, blocks[3])
    relay_in(rel, relsem, 1)
    for g in range(1, KVH):
        relay_out(sends, p, rel, kvs, rsem, g, up, blocks[3])
    for g in range(2, KVH):
        for kind in range(2):
            s = 2 + kind - core
            sends.start("near", x <= 2, slot(kind, 0, g), slot(kind, s, g), rsem.at[kind, s - 1, g],
                        p.at(x=x + 1, core=kind), blocks[8])
    for side in (up, down):
        signal(None, ready2, p.at(zh=side))

    def forward(g):
        for s in (1, 2):
            pl.when(core == 0)(lambda: arrived(slot(0, s, g), rsem.at[0, s - 1, g]))
            pl.when(core == 1)(lambda: arrived(slot(1, s + 1, g), rsem.at[1, s, g]))
            sends.start("core0", core0, slot(0, s, g), slot(0, s + 1, g), rsem.at[0, s, g],
                        p.at(core=1), blocks[24])
            sends.start("core1", core1, slot(1, s + 1, g), slot(1, s, g), rsem.at[1, s - 1, g],
                        p.at(core=0), blocks[24])
            if s == 1:
                sends.start("f3k", on0, slot(0, 1, g), slot(0, 3, g), rsem.at[0, 2, g],
                            p.at(x=x + 1, core=0), blocks[4])
                sends.start("f3v", on1, slot(1, 2, g), slot(1, 3, g), rsem.at[1, 2, g],
                            p.at(x=x + 1, core=0), blocks[4])

    def slots_ready(g):
        @pl.when(core == 0)
        def _():
            arrived(slot(0, 3, g), rsem.at[0, 2, g])
            for s in (1, 2, 3):
                arrived(slot(1, s, g), rsem.at[1, s - 1, g])

        @pl.when(core == 1)
        def _():
            arrived(slot(1, 1, g), rsem.at[1, 0, g])
            for s in (1, 2, 3):
                arrived(slot(0, s, g), rsem.at[0, s - 1, g])

    def compute(g):
        keys = kvs[0, g]
        values = kvs[1, g]
        q_all = jnp.concatenate([qv[:, lanes_of(8 * g + h)] for h in range(8)], axis=0)
        do_all = jnp.concatenate([dov[:, lanes_of(8 * g + h)] for h in range(8)], axis=0)
        mask = jnp.concatenate([bias[...], bias[...]], axis=1)
        probs, dscores = [], []
        for pair in range(4):
            cut = slice(pair * 2 * TOK, (pair + 1) * 2 * TOK)
            s = dot(keys, q_all[cut], 1, 1) * (SCALE * LOG2E) + mask
            dp = dot(values, do_all[cut], 1, 1)
            m = jnp.max(s, axis=0, keepdims=True)
            w = jnp.exp2(s - m)
            total = jnp.sum(w, axis=0, keepdims=True)
            mixed = jnp.sum(w * dp, axis=0, keepdims=True)
            inv = 1.0 / total
            delta = mixed * inv
            prob = w * inv
            probs.append(prob.astype(BF))
            dscores.append((prob * (dp - delta)).astype(BF))
        pb = jnp.concatenate(probs, axis=1)
        ds = jnp.concatenate(dscores, axis=1)
        dkv[1, g] = dot(pb, do_all, 1, 0).astype(BF)
        dkv[0, g] = (dot(ds, q_all, 1, 0) * SCALE).astype(BF)
        home1(g)
        ot = dot(jnp.transpose(values), pb, 1, 0).astype(BF)
        dqt = (dot(jnp.transpose(keys), ds, 1, 0) * SCALE).astype(BF)
        for h in range(8):
            oh = ot[:, h * TOK:(h + 1) * TOK]
            ov[:, lanes_of(8 * g + h)] = jnp.transpose(oh)
            dqv[:, lanes_of(8 * g + h)] = jnp.transpose(dqt[:, h * TOK:(h + 1) * TOK])
            gram[h % 2, 4 * g + h // 2] = dot(oh, oh, 1, 1).astype(BF)
        heads = lanes_of(8 * g, 8)
        local_copy(None, ov.at[:, heads], attn_hbm.at[:, heads], outsem.at[0])
        local_copy(None, dqv.at[:, heads], dq_hbm.at[:, heads], outsem.at[1])

    def part(kind, s, g):
        return dkv.at[kind, g, pl.ds(s * TOK, TOK), :]

    def home1(g):
        for i in range(2):
            sends.start("core0", core0, part(1, 1 + i, g), mate.at[i, g], msem.at[i, g], p.at(core=1), blocks[24])
            sends.start("core1", core1, part(0, 2 + i, g), mate.at[i, g], msem.at[i, g], p.at(core=0), blocks[24])
        for kind in range(2):
            for j in range(4):
                piece = dkv.at[kind, g, pl.ds(3 * TOK + j * QUARTER, QUARTER), :]
                for sx, b in ((0, 2), (1, 3)):
                    here = tail_at[sx]
                    if kind == 0 and j == sx:
                        local_copy(here, piece, rel2.at[b, g], rel2sem.at[b, g])
                    else:
                        sends.start(("tail", sx), here, piece, rel2.at[b, g], rel2sem.at[b, g],
                                    p.at(x=j, core=kind), blocks[7])
            sends.start("core1", core1, part(kind, 1, g), in2.at[kind, g], in2sem.at[kind, g], p.at(core=0), blocks[24])
            sends.start("m3", two_up, part(kind, 3, g), in2.at[kind, g],
                        in2sem.at[kind, g], p.at(x=x - 2, core=1), blocks[8])

    def home2(g):
        for i in range(2):
            arrived(mate.at[i, g], msem.at[i, g])
            rows = pl.ds(pl.multiple_of((1 + i + core) * TOK, TOK), TOK)
            mine = dkv[core, g, rows, :]
            snd[i, g] = (mine.astype(F32) + mate[i, g].astype(F32)).astype(BF)
            sends.start("n", x_up, snd.at[i, g], in1.at[core, g], in1sem.at[core, g],
                        p.at(x=x - 1, core=1 - i), blocks[8])
            for j in range(4):
                piece = snd.at[i, g, pl.ds(j * QUARTER, QUARTER), :]
                if j == 0:
                    local_copy(x0, piece, rel2.at[i, g], rel2sem.at[i, g])
                else:
                    sends.start("r", x0, piece, rel2.at[i, g], rel2sem.at[i, g], p.at(x=j), blocks[6])

    def home3(g):
        def there(ref):
            return ref.at[core, g, rows_of(x), :]

        arrived(rel2.at[2, g], rel2sem.at[2, g])
        sends.start("home", None, rel2.at[2, g], there(in2), in2sem.at[core, g], p.at(x=2, core=1, zh=down), blocks[3])
        arrived(rel2.at[1, g], rel2sem.at[1, g])
        sends.start("home", None, rel2.at[1, g], there(in1), in1sem.at[core, g], p.at(x=3, core=0, zh=down), blocks[3])
        arrived(rel2.at[0, g], rel2sem.at[0, g])
        arrived(rel2.at[3, g], rel2sem.at[3, g])
        relsum[g] = (
            rel2[0, g].astype(F32) + rel2[3, g].astype(F32)).astype(BF)
        sends.start("home", None, relsum.at[g], there(in1), in1sem.at[core, g], p.at(x=3, core=1, zh=down), blocks[3])

    last = both(x == 3, core == 1)
    outs = (dk_ref, dv_ref)

    def home4(g):
        for kind in range(2):
            arrived(in1.at[kind, g], in1sem.at[kind, g])
            near = dkv[kind, g, pl.ds(0, TOK), :].astype(F32) + in1[kind, g].astype(F32)

            @pl.when(last)
            def _():
                outs[kind][0, :, lanes_of(g)] = near.astype(BF)

            @pl.when(jnp.logical_not(last))
            def _():
                arrived(in2.at[kind, g], in2sem.at[kind, g])
                outs[kind][0, :, lanes_of(g)] = (near + in2[kind, g].astype(F32)).astype(BF)

            zown[g, :, pl.ds(kind * HD, HD)] = outs[kind][0, :, lanes_of(g)]

    def factor1(g):
        z = zown[g]
        ordered = dot(z, order[...], 1, 0).astype(BF)
        cs[g] = dot(ordered, z, 0, 0).reshape(2, 128, 2 * HD).astype(BF)
        sends.start("gc", None, cs.at[g, other], cr.at[g], gsem.at[g, 0], p.at(core=other), blocks[8])

    def factor2(g):
        arrived(cr.at[g], gsem.at[g, 0])
        ys[g] = (cs[g, core].astype(F32) + cr[g].astype(F32)).reshape(4, 32, 2 * HD).astype(BF)
        for j in (1, 2, 3):
            sends.start("gy", None, ys.at[g, ring(y, j)], yr.at[g, j - 1], gsem.at[g, 1], p.at(y=ring(y, j)), blocks[6])

    def factor3(g):
        arrived(yr.at[g], gsem.at[g, 1])
        total = ys[g, y].astype(F32)
        for j in range(3):
            total = total + yr[g, j].astype(F32)
        xs[g] = total.reshape(4, 8, 2 * HD)
        for j in (1, 2, 3):
            sends.start("gx", None, xs.at[g, ring(x, j)], xr.at[g, j - 1], gsem.at[g, 2], p.at(x=ring(x, j)), blocks[3])

    def factor4(g):
        arrived(xr.at[g], gsem.at[g, 2])
        total = xs[g, x]
        for j in range(3):
            total = total + xr[g, j]
        mine = zh * 4 + zl
        for j in range(4):
            zs[g, j] = total[2 * j:2 * j + 2, :]
            here = both(zh == g, zl == j)
            sends.start("gz", jnp.logical_not(here), zs.at[g, j], zr.at[mine], zsem.at[0],
                        p.at(zh=g, zl=j), all_z)
            local_copy(here, zs.at[g, j], zr.at[mine], zsem.at[0])

    def out1(g):
        mine = pl.ds(4 * g, 4)
        sends.start("oc", None, gram.at[other, mine], g0.at[mine], o0sem.at[g], p.at(core=other), blocks[16])

    def out2(g):
        arrived(g0.at[pl.ds(4 * g, 4)], o0sem.at[g])
        for h in range(4):
            pair_sum = gram[core, 4 * g + h].astype(F32) + g0[4 * g + h].astype(F32)
            split = pair_sum.reshape(4, 4, 8, HD)
            for j in range(4):
                ay[g, j, pl.ds(h * 32, 32), :] = split[:, j].reshape(32, HD).astype(BF)
        for j in (1, 2, 3):
            sends.start("oy", None, ay.at[g, ring(y, j)], ry.at[g, j - 1], oysem.at[g], p.at(y=ring(y, j)), blocks[12])

    def out3(g):
        arrived(ry.at[g], oysem.at[g])
        total = ay[g, y].astype(F32)
        for j in range(3):
            total = total + ry[g, j].astype(F32)
        ax[g] = total.reshape(4, 32, HD).astype(BF)
        for j in (1, 2, 3):
            sends.start("ox", None, ax.at[g, ring(x, j)], rx.at[g, j - 1], oxsem.at[g], p.at(x=ring(x, j)), blocks[3])

    def out4(g):
        arrived(rx.at[g], oxsem.at[g])
        total = ax[g, x].astype(F32)
        for j in range(3):
            total = total + rx[g, j].astype(F32)
        total = total.reshape(4, 8, HD)
        for j in range(4):
            az[j, g] = total[j]

    forward(0)

    def step(g, _):
        pl.when(g < 3)(lambda: forward(jnp.minimum(g + 1, 3)))
        slots_ready(g)
        heads = lanes_of(8 * g, 8)
        arrived(qv.at[:, heads], qsem.at[0, g])
        arrived(dov.at[:, heads], qsem.at[1, g])
        compute(g)
        out1(g)

        @pl.when(g >= 1)
        def _():
            home2(g - 1)
            out2(g - 1)

        @pl.when(g >= 2)
        def _():
            home3(g - 2)
            out3(g - 2)

        @pl.when(g == 3)
        def _():
            home4(0)
            factor1(0)
            out4(0)
        return 0

    lax.fori_loop(0, KVH, step, 0)
    home2(3)
    home3(2)
    out2(3)
    out3(2)
    pl.semaphore_wait(ready2, 2)
    for j in (1, 2, 3):
        signal(None, ready3, p.at(zl=ring(zl, j)))
    home4(1)
    factor1(1)
    home3(3)
    factor2(0)
    out4(1)
    out3(3)
    home4(2)
    factor1(2)
    factor2(1)
    factor3(0)
    out4(2)
    out4(3)
    for j in (1, 2, 3):
        sends.start("oz", None, az.at[ring(zl, j)], rz.at[j - 1], ozsem.at[0], p.at(zl=ring(zl, j)), rz)
    home4(3)
    factor1(3)
    factor2(2)
    factor3(1)
    pl.semaphore_wait(ready3, 3)
    factor4(0)
    factor2(3)
    factor3(2)
    factor4(1)
    arrived(rz, ozsem.at[0])
    ah[...] = az[zl] + rz[0] + rz[1] + rz[2]
    for j in (1, 2, 3):
        sends.start("oh", None, ah.at[ring(zh, j)], rh.at[j - 1], ozsem.at[1], p.at(zh=ring(zh, j)), rh)
    factor3(3)
    factor4(2)
    factor4(3)
    arrived(attn_hbm, outsem.at[0])
    arrived(dq_hbm, outsem.at[1])
    tokens = float(512 * TOK)
    arrived(rh, ozsem.at[1])
    of_ref[...] = (ah[zh] + rh[0] + rh[1] + rh[2]) / tokens
    sends.finish()
    total = jnp.zeros((2, 2 * HD), F32)
    arrived(zr, zsem.at[0])
    for j in range(16):
        total = total + zr[j]
    gf_ref[...] = total / tokens


def relay_in(rel, relsem, wide):
    group = pl.ds(0, 1) if wide == 0 else pl.ds(1, 3)
    for b in range(3):
        arrived(rel.at[b, group], relsem.at[b, wide])


def relay_out(sends, p, rel, kvs, rsem, g, up, relayed):
    for b in range(3):
        s = (3 - b) + (0 if b == 0 else p.core)
        rows = pl.ds(pl.multiple_of(s * TOK + p.x * QUARTER, QUARTER), QUARTER)
        sends.start("relay", None, rel.at[b, g], kvs.at[p.core, g, rows, :],
                    rsem.at[p.core, s - 1, g], p.at(x=0, zh=up, core=0 if b == 0 else p.core), relayed)


def fused(order, q, do, keys, values):
    vmem, hbm = pl.BlockSpec(memory_space=pltpu.VMEM), pl.BlockSpec(memory_space=pl.ANY)
    wide, all_lanes = KVH * HD, q.shape[1]
    V = pltpu.VMEM
    D = pltpu.SemaphoreType.DMA
    return pl.pallas_call(
        fused_kernel,
        out_shape=[
            jax.ShapeDtypeStruct((TOK, all_lanes), BF),
            jax.ShapeDtypeStruct((TOK, all_lanes), BF),
            jax.ShapeDtypeStruct((1, TOK, wide), BF),
            jax.ShapeDtypeStruct((1, TOK, wide), BF),
            jax.ShapeDtypeStruct((8, HD), F32),
            jax.ShapeDtypeStruct((2, 2 * HD), F32),
        ],
        in_specs=[hbm] * 5,
        out_specs=[hbm, hbm] + [vmem] * 4,
        scratch_shapes=[
            pltpu.SMEM(order.shape, order.dtype),
            V((TOK, all_lanes), BF), V((TOK, all_lanes), BF), V((TOK, all_lanes), BF), V((TOK, all_lanes), BF),
            V((2, KVH, STEPS * TOK, HD), BF), V((2, KVH, STEPS * TOK, HD), BF),
            V((2, 16, HD, HD), BF), V((STEPS * TOK, TOK), F32),
            V((3, KVH, QUARTER, HD), BF), V((2, KVH, TOK, HD), BF), V((2, KVH, TOK, HD), BF),
            V((4, KVH, QUARTER, HD), BF), V((KVH, QUARTER, HD), BF), V((2, KVH, TOK, HD), BF), V((2, KVH, TOK, HD), BF),
            V((16, HD, HD), BF), V((4, 4, 128, HD), BF), V((4, 3, 128, HD), BF),
            V((4, 4, 32, HD), BF), V((4, 3, 32, HD), BF),
            V((4, 4, 8, HD), F32), V((3, 4, 8, HD), F32), V((4, 8, HD), F32), V((3, 8, HD), F32),
            V((4, TOK, 2 * HD), BF), V((2 * HD, 2 * HD), BF),
            V((4, 2, 128, 2 * HD), BF), V((4, 128, 2 * HD), BF),
            V((4, 4, 32, 2 * HD), BF), V((4, 3, 32, 2 * HD), BF),
            V((4, 4, 8, 2 * HD), F32), V((4, 3, 8, 2 * HD), F32),
            V((4, 4, 2, 2 * HD), F32), V((16, 2, 2 * HD), F32),
            D((24,)), D((2, 4)), D((1,)), D((2,)), D((2,)), D((2, 3, 4)), D((3, 2)), D((2, 4)), D((4, 4)), D((2, 4)), D((2, 4)),
            D((4,)), D((4,)), D((4,)), D((2,)), D((4, 3)), D((1,)),
            pltpu.SemaphoreType.REGULAR, pltpu.SemaphoreType.REGULAR, pltpu.SemaphoreType.REGULAR,
        ],
        compiler_params=pltpu.CompilerParams(
            collective_id=0, has_side_effects=True, vmem_limit_bytes=60 * 2**20),
    )(order, q, do, keys, values)


def handover_kernel(*refs):
    count = len(refs) // 2
    for i in range(count):
        refs[count + i][...] = refs[i][...]


def handover(attn, dq, dk, dv, out_factor, grad_factor):
    arrays = (attn, dq, dk, dv, out_factor, grad_factor)
    steps = 2
    big = pl.BlockSpec((TOK // steps, attn.shape[1]), lambda i: (i, 0))
    small = pl.BlockSpec((1, TOK // steps, dk.shape[2]), lambda i: (0, i, 0))
    whole = [pl.BlockSpec(a.shape, lambda i: (0, 0)) for a in (out_factor, grad_factor)]
    specs = [big, big, small, small] + whole
    return pl.pallas_call(
        handover_kernel,
        grid=(steps,),
        out_shape=[jax.ShapeDtypeStruct(a.shape, a.dtype) for a in arrays],
        in_specs=specs,
        out_specs=specs,
    )(*arrays)


def local(queries, key_heads, value_heads, out_grad, block_order):
    outs = fused(block_order, queries[0], out_grad[0], key_heads[0], value_heads[0])
    attn, dq, dk, dv, out_factor, grad_factor = handover(*outs)
    return attn[None], dq[None], dk, dv, out_factor, grad_factor


def solution(mesh):
    rows = P("dp", "ctx", None)
    return jax.shard_map(
        local,
        mesh=mesh,
        in_specs=(rows, rows, rows, rows, P()),
        out_specs=(rows, rows, rows, rows, P(("ctx", "dp"), None), P(("ctx", "dp"), None)),
        check_vma=False,
    )
```
